32 devices in a mesh: dp: 4 (over x, core), expert: 8 (over z, y).
Axes of the slice: x: 2, y: 2, z: 4, core: 2. Of those that a mesh axis runs over, the one named last changes fastest.
Arguments:
- query: bfloat16 [2, 2048, 2560], P(None, ('dp', 'expert')), may hold values from -24 to 24
- keys: bfloat16 [2, 2048, 512], P(None, ('dp', 'expert')), may hold values from -4 to 4
- values: bfloat16 [2, 2048, 512], P(None, ('dp', 'expert')), may hold values from -6 to 6
- lengths: int32 [2, 32, 4], P(None, ('dp', 'expert')), may hold values from 0 to 64, as said below
- routes: int32 [2, 2048, 6], P(None, ('dp', 'expert')), may hold values from 0 to 7, as said below
- gates: float32 [2, 2048, 6], P(None, ('dp', 'expert')), may hold values from 0.05 to 0.4
- norm_gain: float32 [2560], replicated, may hold values from 0.1 to 1.9
- old_holds: int32 [8], replicated, may hold values from 0 to 7, as said below
- dup_experts: int32 [4], replicated, may hold values from 0 to 7, as said below
- w_gate: bfloat16 [8, 2560, 768], P('expert'), may hold values from -0.125 to 0.125
- w_up: bfloat16 [8, 2560, 768], P('expert'), may hold values from -0.125 to 0.125
- w_down: bfloat16 [8, 768, 2560], P('expert'), may hold values from -0.21875 to 0.21875
Outputs:
- layer_out: bfloat16 [2, 2048, 2560], P(None, ('dp', 'expert'))
The draws below stay inside these ranges and needn't reach their ends.
Inputs may be any that keep to these rules, and one draw needn't show every extreme that they name: Each length is a multiple of 8; the 4 lengths of one device in one batch add up to 64. `routes`: each token names 6 different experts. `dup_experts`: 4 different experts. `old_holds`: each expert stands in exactly one slot.
All inputs are finite; a program needn't handle non-finite values.
Results may differ from the reference program's by a relative error of at most 0.0061.
Values may be sent and summed in bfloat16 or wider, within the bound.
No kernel may reach another device: no remote copies, remote signals or barrier semaphores. Data moves between devices by JAX's collectives and lax.ppermute only.
A program may use at most 128 MiB of HBM per device.

```python
import jax
import jax.numpy as jnp
from jax import lax

D = 2560
QUERY_HEAD_COUNT = 20
SHARED_KV_HEADS = 4
HEAD_WIDTH = 128
TOPK = 6
FFW = 768
NDUP = 4
REQ = 4
TOK = 64
EXPERTS = 8
BATCH_TOKENS = 2048
CAP = 6


def drawn_pair(key):
    base_query = jax.random.fold_in(key, 101)
    base_keys = jax.random.fold_in(key, 102)
    query_shape = (2, BATCH_TOKENS, QUERY_HEAD_COUNT * HEAD_WIDTH)
    key_layout = (2, BATCH_TOKENS, SHARED_KV_HEADS * HEAD_WIDTH)
    query = jnp.clip(jax.random.normal(base_query, query_shape, jnp.float32), -4.0, 4.0)
    keys = jnp.clip(jax.random.normal(base_keys, key_layout, jnp.float32), -4.0, 4.0)
    return (query.astype(jnp.bfloat16), keys.astype(jnp.bfloat16))


def draw_query(key, part):
    return drawn_pair(key)[0]


def draw_keys(key, part):
    return drawn_pair(key)[1]


def draw_lengths(key, part):
    units = TOK // 8
    count = BATCH_TOKENS // TOK
    cuts = jax.random.randint(jax.random.fold_in(key, 301), (2, count, REQ - 1), 0, units + 1)
    cuts = jnp.sort(cuts, axis=-1)
    device = lax.iota(jnp.int32, count)
    cuts = jnp.where((device == 0)[None, :, None], units, cuts)
    edges = jnp.concatenate([jnp.zeros((2, count, 1), jnp.int32), cuts.astype(jnp.int32), jnp.full((2, count, 1), units, jnp.int32)], axis=-1)
    return ((edges[..., 1:] - edges[..., :-1]) * 8).astype(jnp.int32)


def slot_order(key):
    return jax.random.permutation(jax.random.fold_in(key, 201), EXPERTS).astype(jnp.int32)


def hot_set(key):
    order = slot_order(key)
    middle = EXPERTS // 2
    chosen_slots = jnp.array([0, middle - 1, middle, EXPERTS - 1], jnp.int32)
    hot = order[chosen_slots].astype(jnp.int32)
    present = jnp.sum((hot == EXPERTS - 1).astype(jnp.int32)) > 0
    last_pick = jnp.where(present, hot[3], EXPERTS - 1).astype(jnp.int32)
    return hot.at[3].set(last_pick).astype(jnp.int32)


def draw_old_holds(key, part):
    return slot_order(key)


def draw_routes(key, part):
    hot = hot_set(key)
    expert_list = lax.iota(jnp.int32, EXPERTS)
    router_logits = jax.random.randint(jax.random.fold_in(key, 202), (2, BATCH_TOKENS, EXPERTS), 0, 2 ** 20) * EXPERTS
    router_logits = router_logits + expert_list[None, None, :]
    selected_experts = hot[lax.iota(jnp.int32, BATCH_TOKENS) % NDUP]
    extra_reward = (selected_experts[:, None] == expert_list[None, :]).astype(jnp.int32) * 2 ** 27
    router_logits = router_logits + extra_reward[None]
    _, picked = lax.top_k(router_logits, TOPK)
    return picked.astype(jnp.int32)


def draw_dup_experts(key, part):
    return hot_set(key)


def block_scale(key, dims, shards, smallest, largest):
    level = 1.0
    for axis_at, blocks in shards:
        steps = jax.random.uniform(jax.random.fold_in(jax.random.fold_in(key, 6), axis_at), (blocks,), jnp.float32, smallest / len(shards), largest / len(shards))
        level = level * jnp.repeat(jnp.exp(steps), dims[axis_at] // blocks).reshape((-1,) + (1,) * (len(dims) - 1 - axis_at))
    return level


def gaussian(rng, dims, scale, reach, cuts=(), kind=jnp.bfloat16):
    level = block_scale(rng, dims, cuts, -0.22, 0.18) if cuts else 1.0
    values = jax.random.normal(rng, dims, jnp.float32) * scale * level
    return jnp.minimum(jnp.maximum(values, -reach), reach).astype(kind)


def setup_inputs(seed: int = 0) -> dict:
    key_of = jax.random.split(jax.random.key(seed), 13)
    query = draw_query(jax.random.fold_in(key_of[12], 71), 0)
    keys = draw_keys(jax.random.fold_in(key_of[12], 71), 0)
    values = gaussian(key_of[2], (2, BATCH_TOKENS, SHARED_KV_HEADS * HEAD_WIDTH), 1.0, 6.0, ((1, 32),))
    lengths = draw_lengths(jax.random.fold_in(key_of[12], 71), 0)
    routes = draw_routes(jax.random.fold_in(key_of[12], 71), 0)
    gates = jnp.clip(0.05 + 0.35 * jax.random.uniform(key_of[5], (2, BATCH_TOKENS, TOPK), jnp.float32) ** block_scale(key_of[5], (2, BATCH_TOKENS, TOPK), ((1, 32),), -0.2, 0.2), 0.05, 0.4)
    norm_gain = jnp.clip(1.0 + 0.18 * jax.random.normal(key_of[6], (D,), jnp.float32), 0.1, 1.9)
    old_holds = draw_old_holds(jax.random.fold_in(key_of[12], 71), 0)
    dup_experts = draw_dup_experts(jax.random.fold_in(key_of[12], 71), 0)
    w_gate = gaussian(key_of[9], (EXPERTS, D, FFW), D ** -0.5, 0.125, ((0, 8),))
    w_up = gaussian(key_of[10], (EXPERTS, D, FFW), D ** -0.5, 0.125, ((0, 8),))
    w_down = gaussian(key_of[11], (EXPERTS, FFW, D), FFW ** -0.5, 0.21875, ((0, 8),))
    return dict(query=query, keys=keys, values=values, lengths=lengths, routes=routes, gates=gates, norm_gain=norm_gain, old_holds=old_holds, dup_experts=dup_experts, w_gate=w_gate, w_up=w_up, w_down=w_down)


def attend(query, key_rows, value_rows, lengths):
    rows = query.shape[0]
    kv_heads = key_rows.shape[1] // HEAD_WIDTH
    query_group = query.shape[1] // HEAD_WIDTH // kv_heads
    ends = jnp.cumsum(lengths)
    position = lax.iota(jnp.int32, rows)
    request = lax.optimization_barrier(jnp.sum((position[:, None] >= ends[None, :]).astype(jnp.int32), axis=1))
    allowed = (request[:, None] == request[None, :]) & (position[None, :] <= position[:, None])
    query_heads = query.reshape(rows, kv_heads, query_group, HEAD_WIDTH).astype(jnp.float32)
    key_heads = key_rows.reshape(rows, kv_heads, HEAD_WIDTH).astype(jnp.float32)
    value_heads = value_rows.reshape(rows, kv_heads, HEAD_WIDTH).astype(jnp.float32)
    router_logits = jnp.einsum('qhgd,khd->hgqk', query_heads, key_heads) * HEAD_WIDTH ** (-0.5)
    router_logits = jnp.where(allowed[None, None], router_logits, -1e+30)
    highest = lax.optimization_barrier(jnp.max(router_logits, axis=-1, keepdims=True))
    weights = jnp.exp(router_logits - highest)
    probs = (weights / lax.optimization_barrier(jnp.sum(weights, axis=-1, keepdims=True))).astype(jnp.bfloat16)
    mixed = jnp.einsum('hgqk,khd->qhgd', probs.astype(jnp.float32), value_heads)
    return mixed.reshape(rows, kv_heads * query_group * HEAD_WIDTH)

def normalize(attn, gain):
    meansq = lax.optimization_barrier(jnp.mean(attn * attn, axis=-1, keepdims=True))
    return (attn * lax.rsqrt(meansq + 1e-05) * gain).astype(jnp.bfloat16)

def expert_rows(rows, gate_mat, up_mat, down_mat):
    gate_val = jnp.dot(rows, gate_mat, preferred_element_type=jnp.float32)
    up_val = jnp.dot(rows, up_mat, preferred_element_type=jnp.float32)
    hidden = (jax.nn.silu(gate_val) * up_val).astype(jnp.bfloat16)
    return jnp.dot(hidden, down_mat, preferred_element_type=jnp.float32).astype(jnp.bfloat16)

def positions(routes, copies_of):
    expert_list = lax.iota(jnp.int32, copies_of.shape[0])
    hit = (routes[:, :, None] == expert_list[None, None, :]).astype(jnp.int32)
    named = lax.optimization_barrier(jnp.sum(hit, axis=1))
    before = jnp.cumsum(named, axis=0) - named
    place = lax.optimization_barrier(jnp.sum(hit * before[:, None, :], axis=2))
    limit = lax.optimization_barrier(jnp.sum(hit * copies_of[None, None, :], axis=2))
    return (place, place < limit * CAP)

def block_attention(parts):
    return attend(parts[0], parts[1], parts[2], parts[3])

def one_batch(query, keys, values, lengths, routes, gates, gain, holder, copies_of, w_gate, w_up, w_down):
    count = BATCH_TOKENS // TOK
    attn = lax.map(block_attention, (query.reshape(count, TOK, -1), keys.reshape(count, TOK, -1), values.reshape(count, TOK, -1), lengths))
    attn = attn.reshape(BATCH_TOKENS, -1)
    normed = normalize(attn, gain)
    block_routes = routes.reshape(count, TOK, TOPK)
    place, kept = jax.vmap(lambda selected_experts: positions(selected_experts, copies_of))(block_routes)
    source = lax.iota(jnp.int32, count)[:, None, None]
    row_index = lax.iota(jnp.int32, TOK)[None, :, None]
    width = count * 2 * CAP
    column = source * (2 * CAP) + place
    expert = jnp.where(kept, block_routes, EXPERTS)
    token = jnp.broadcast_to(source * TOK + row_index, place.shape).astype(jnp.int32)
    table_rows = jnp.full((EXPERTS, width), BATCH_TOKENS, jnp.int32).at[expert, column].set(token, mode='drop')
    table_gate = jnp.zeros((EXPERTS, width), jnp.float32).at[expert, column].set(gates.reshape(count, TOK, TOPK), mode='drop')
    padded = jnp.concatenate([normed, jnp.zeros((1, normed.shape[1]), normed.dtype)], axis=0)

    def step(total, index):
        slot = holder[index]
        picked = table_rows[index]
        rows = padded[picked]
        result = expert_rows(rows, w_gate[slot], w_up[slot], w_down[slot])
        total = total.at[picked].add(table_gate[index][:, None] * result.astype(jnp.float32))
        return (total, None)
    total, _ = lax.scan(step, jnp.zeros((BATCH_TOKENS + 1, normed.shape[1]), jnp.float32), lax.iota(jnp.int32, EXPERTS))
    return (attn + total[:BATCH_TOKENS]).astype(jnp.bfloat16)

def reference(query, keys, values, lengths, routes, gates, norm_gain, old_holds, dup_experts, w_gate, w_up, w_down):
    expert_list = lax.iota(jnp.int32, EXPERTS)
    holder = lax.optimization_barrier(jnp.sum(expert_list[:, None] * (old_holds[:, None] == expert_list[None, :]).astype(jnp.int32), axis=0))
    doubled = lax.optimization_barrier(jnp.sum((dup_experts[:, None] == expert_list[None, :]).astype(jnp.int32), axis=0))
    first = one_batch(query[0], keys[0], values[0], lengths[0], routes[0], gates[0], norm_gain, holder, jnp.ones_like(doubled), w_gate, w_up, w_down)
    second = one_batch(query[1], keys[1], values[1], lengths[1], routes[1], gates[1], norm_gain, holder, 1 + doubled, w_gate, w_up, w_down)
    return jnp.stack([first, second])
```

```python
import functools

import jax
import jax.numpy as jnp
from jax import lax
from jax.experimental import pallas as pl
from jax.experimental.pallas import tpu as pltpu
from jax.sharding import PartitionSpec as P

HEAD_WIDTH = 128
CAP = 6
PACK = 8
SPLIT = CAP // (PACK - CAP)
GROUPS = 3
VMEM_LIMIT = 56 * 1024 * 1024

F32 = jnp.float32
BF16 = jnp.bfloat16


def dot(a, b, dims=((1,), (0,))):
    return lax.dot_general(a, b, (dims, ((), ())), preferred_element_type=F32)


def row_iota(shape, axis):
    return lax.broadcasted_iota(jnp.int32, shape, axis)


def count_steps(value, step, upto):
    total = jnp.zeros_like(value)
    for at in range(1, upto):
        total = total + (value >= step * at).astype(jnp.int32)
    return total


def slot_picks(width, holds_ref, dup_ref, routes_ref):
    _, batches, tokens = routes_ref.shape
    lanes = batches * tokens
    rows = width * GROUPS * PACK
    shape = (rows, lanes)
    row = row_iota(shape, 0)
    lane = row_iota(shape, 1)
    slot = count_steps(row, GROUPS * PACK, width)
    within = row - slot * (GROUPS * PACK)
    group = count_steps(within, PACK, GROUPS)
    place = within - group * PACK
    expert = jnp.zeros(shape, jnp.int32)
    for at in range(width):
        expert = jnp.where(slot == at, holds_ref[at], expert)
    doubled = jnp.zeros(shape, jnp.bool_)
    for at in range(dup_ref.shape[0]):
        doubled = doubled | (expert == dup_ref[at])
    batch = (lane >= tokens).astype(jnp.int32)
    allowed = (batch == (group >= 1).astype(jnp.int32)) & (doubled | (group < 2))
    routes = routes_ref[...]
    routes = jnp.concatenate([routes[:, at, :] for at in range(batches)], axis=1)
    named = [routes[k : k + 1, :] == expert for k in range(routes.shape[0])]
    hit = functools.reduce(jnp.logical_or, named)
    earlier = row_iota((lanes, lanes), 0)
    later = row_iota((lanes, lanes), 1)
    same = (earlier >= tokens) == (later >= tokens)
    before_mat = jnp.where((earlier < later) & same, 1.0, 0.0).astype(BF16)
    before = dot(jnp.where(hit, 1.0, 0.0).astype(BF16), before_mat).astype(jnp.int32)
    before = before - jnp.where(group == 2, CAP, 0)
    live = hit & allowed
    lead = live & (place < CAP) & (before == place)
    trail = [
        live & (place >= CAP) & (before == (place - CAP) * SPLIT + piece) for piece in range(SPLIT)
    ]
    return lead, trail, named


def attend(query_ref, key_ref, value_ref, lengths_ref, batch, attn_ref):
    tokens = query_ref.shape[1]
    kv_heads = key_ref.shape[2] // HEAD_WIDTH
    group = query_ref.shape[2] // HEAD_WIDTH // kv_heads
    at_row = row_iota((tokens, tokens), 0)
    at_col = row_iota((tokens, tokens), 1)
    row_request = jnp.zeros((tokens, tokens), jnp.int32)
    col_request = jnp.zeros((tokens, tokens), jnp.int32)
    end = jnp.int32(0)
    for r in range(lengths_ref.shape[2]):
        end = end + lengths_ref[batch, 0, r]
        row_request = row_request + (at_row >= end).astype(jnp.int32)
        col_request = col_request + (at_col >= end).astype(jnp.int32)
    allowed = (row_request == col_request) & (at_col <= at_row)
    squares = jnp.zeros((tokens, HEAD_WIDTH), F32)
    for h in range(kv_heads):
        kv = slice(h * HEAD_WIDTH, (h + 1) * HEAD_WIDTH)
        heads = [
            slice((h * group + g) * HEAD_WIDTH, (h * group + g + 1) * HEAD_WIDTH)
            for g in range(group)
        ]
        q = jnp.concatenate([query_ref[batch, :, cols] for cols in heads], axis=0)
        scores = dot(q, key_ref[batch, :, kv], ((1,), (1,))) * HEAD_WIDTH ** (-0.5)
        scores = scores.reshape(group, tokens, tokens)
        scores = jnp.where(allowed[None], scores, -1e30)
        weights = jnp.exp(scores - jnp.max(scores, axis=-1, keepdims=True))
        probs = (weights / jnp.sum(weights, axis=-1, keepdims=True)).astype(BF16)
        mixed = dot(probs.reshape(group * tokens, tokens), value_ref[batch, :, kv])
        for g, cols in enumerate(heads):
            part = mixed[g * tokens : (g + 1) * tokens]
            attn_ref[batch, :, cols] = part
            squares = squares + part * part
    meansq = jnp.sum(squares, axis=-1, keepdims=True) / query_ref.shape[2]
    return lax.rsqrt(meansq + 1e-05)


def front_kernel(
    lengths_ref,
    holds_ref,
    dup_ref,
    query_ref,
    key_ref,
    value_ref,
    routes_ref,
    gain_ref,
    attn_ref,
    send_ref,
    normed_ref,
):
    batches, tokens, features = query_ref.shape
    cols = send_ref.shape[1]
    step = cols // SPLIT
    for b in range(batches):
        scale = attend(query_ref, key_ref, value_ref, lengths_ref, b, attn_ref)
        normed_ref[b * tokens : (b + 1) * tokens, :] = (
            attn_ref[b] * scale * gain_ref[...]
        ).astype(BF16)
    width = send_ref.shape[0] // (GROUPS * PACK)
    lead, trail, _ = slot_picks(width, holds_ref, dup_ref, routes_ref)
    tail = normed_ref[:, cols:features]
    for j in range(SPLIT):
        at = slice(j * step, (j + 1) * step)
        picks = jnp.concatenate([lead, trail[j]], axis=1)
        picks = jnp.where(picks, 1.0, 0.0).astype(BF16)
        source = jnp.concatenate([normed_ref[:, at], tail], axis=0)
        send_ref[:, at] = dot(picks, source).astype(BF16)


def weights_kernel(holds_ref, dup_ref, routes_ref, gates_ref, mix_ref):
    width = mix_ref.shape[1] // (GROUPS * PACK)
    lead, trail, named = slot_picks(width, holds_ref, dup_ref, routes_ref)
    gates = gates_ref[...]
    gates = jnp.concatenate([gates[:, at, :] for at in range(gates.shape[1])], axis=1)
    gate = jnp.zeros(lead.shape, F32)
    for k, match in enumerate(named):
        gate = gate + jnp.where(match, gates[k : k + 1, :], 0.0)
    lanes = lead.shape[1]
    for j in range(SPLIT):
        for part, pick in enumerate((lead, trail[j])):
            weight = jnp.where(pick, gate, 0.0)
            high = weight.astype(BF16)
            low = (weight - high.astype(F32)).astype(BF16)
            mix_ref[j, :, (2 * part) * lanes : (2 * part + 1) * lanes] = high
            mix_ref[j, :, (2 * part + 1) * lanes : (2 * part + 2) * lanes] = low


def expert_kernel(got_ref, gate_ref, up_ref, down_ref, back_ref, rows_ref, total_ref):
    rows, cols = got_ref.shape
    features = rows_ref.shape[1]
    step = cols // SPLIT
    chunk = pl.program_id(1)
    shape = (rows, rows)
    row = row_iota(shape, 0)
    other = row_iota(shape, 1)
    tile = row - lax.rem(row, PACK)
    place = row - tile

    def trails(j):
        picked = jnp.zeros(shape, jnp.bool_)
        for a in range(PACK - CAP):
            picked = picked | ((place == a * SPLIT + j) & (other == tile + CAP + a))
        return jnp.where(picked, 1.0, 0.0).astype(BF16)

    @pl.when(chunk == 0)
    def _():
        rows_ref[:, :cols] = got_ref[...]
        tail = jnp.zeros((rows, features - cols), F32)
        for j in range(SPLIT):
            tail = tail + dot(trails(j), got_ref[:, j * step : (j + 1) * step])
        rows_ref[:, cols:] = tail.astype(BF16)
        total_ref[...] = jnp.zeros_like(total_ref)

    gate_val = dot(rows_ref[...], gate_ref[0])
    up_val = dot(rows_ref[...], up_ref[0])
    hidden = (gate_val / (1.0 + jnp.exp(-gate_val)) * up_val).astype(BF16)
    total_ref[...] += dot(hidden, down_ref[0])

    @pl.when(chunk == pl.num_programs(1) - 1)
    def _():
        tail = total_ref[:, cols:].astype(BF16)
        leading = lax.rem(row_iota((rows, step), 0), PACK) < CAP
        for j in range(SPLIT):
            at = slice(j * step, (j + 1) * step)
            moved = dot(trails(j), tail, ((0,), (0,)))
            back_ref[:, at] = jnp.where(leading, total_ref[:, at], moved).astype(BF16)


def combine_kernel(attn_ref, mix_ref, back_ref, out_ref):
    batches, tokens, features = attn_ref.shape
    lanes = batches * tokens
    cols = back_ref.shape[1]
    step = cols // SPLIT
    tail = jnp.zeros((lanes, features - cols), F32)
    for j in range(SPLIT):
        at = slice(j * step, (j + 1) * step)
        mixed = dot(mix_ref[j], back_ref[:, at], ((0,), (0,)))
        lead = mixed[:lanes] + mixed[lanes : 2 * lanes]
        tail = tail + (mixed[2 * lanes : 3 * lanes] + mixed[3 * lanes :])
        for b in range(batches):
            out_ref[b, :, at] = (attn_ref[b, :, at] + lead[b * tokens : (b + 1) * tokens]).astype(
                BF16
            )
    for b in range(batches):
        out_ref[b, :, cols:] = (
            attn_ref[b, :, cols:] + tail[b * tokens : (b + 1) * tokens]
        ).astype(BF16)


def in_vmem(count):
    return [pl.BlockSpec(memory_space=pltpu.VMEM)] * count


def in_smem(count):
    return [pl.BlockSpec(memory_space=pltpu.SMEM)] * count


def exchange(value):
    return lax.all_to_all(value, "expert", split_axis=0, concat_axis=0, tiled=True)


def shards(
    query,
    keys,
    values,
    lengths,
    routes,
    gates,
    norm_gain,
    old_holds,
    dup_experts,
    w_gate,
    w_up,
    w_down,
):
    width = lax.axis_size("expert")
    batches, tokens, features = query.shape
    cols = features * CAP // PACK
    rows = width * GROUPS * PACK
    hidden = w_gate.shape[2]
    params = pltpu.CompilerParams(vmem_limit_bytes=VMEM_LIMIT)
    routes = jnp.transpose(routes, (2, 0, 1))
    gates = jnp.transpose(gates, (2, 0, 1))

    attn, send = pl.pallas_call(
        front_kernel,
        name="attend_and_pack",
        out_shape=(
            jax.ShapeDtypeStruct((batches, tokens, features), F32),
            jax.ShapeDtypeStruct((rows, cols), BF16),
        ),
        in_specs=in_smem(3) + in_vmem(5),
        out_specs=tuple(in_vmem(2)),
        scratch_shapes=[pltpu.VMEM((batches * tokens, features), BF16)],
        compiler_params=params,
    )(lengths, old_holds, dup_experts, query, keys, values, routes, norm_gain.reshape(1, features))

    got = exchange(send)

    mix = pl.pallas_call(
        weights_kernel,
        name="gate_weights",
        out_shape=jax.ShapeDtypeStruct((SPLIT, rows, 4 * batches * tokens), BF16),
        in_specs=in_smem(2) + in_vmem(2),
        out_specs=in_vmem(1)[0],
        compiler_params=params,
    )(old_holds, dup_experts, routes, gates)

    block = GROUPS * PACK * min(width, 8)
    chunk = 256 if hidden % 256 == 0 else hidden
    back = pl.pallas_call(
        expert_kernel,
        name="expert_ffn",
        out_shape=jax.ShapeDtypeStruct((rows, cols), BF16),
        grid=(rows // block, hidden // chunk),
        in_specs=[
            pl.BlockSpec((block, cols), lambda i, j: (i, 0)),
            pl.BlockSpec((1, features, chunk), lambda i, j: (0, 0, j)),
            pl.BlockSpec((1, features, chunk), lambda i, j: (0, 0, j)),
            pl.BlockSpec((1, chunk, features), lambda i, j: (0, j, 0)),
        ],
        out_specs=pl.BlockSpec((block, cols), lambda i, j: (i, 0)),
        scratch_shapes=[
            pltpu.VMEM((block, features), BF16),
            pltpu.VMEM((block, features), F32),
        ],
        compiler_params=params,
    )(got, w_gate, w_up, w_down)

    returned = exchange(back)

    return pl.pallas_call(
        combine_kernel,
        name="combine",
        out_shape=jax.ShapeDtypeStruct((batches, tokens, features), BF16),
        in_specs=in_vmem(3),
        out_specs=in_vmem(1)[0],
        compiler_params=params,
    )(attn, mix, returned)


def solution(mesh):
    placed = (
        P(None, ("dp", "expert"), None),
        P(None, ("dp", "expert"), None),
        P(None, ("dp", "expert"), None),
        P(None, ("dp", "expert"), None),
        P(None, ("dp", "expert"), None),
        P(None, ("dp", "expert"), None),
        P(),
        P(),
        P(),
        P("expert", None, None),
        P("expert", None, None),
        P("expert", None, None),
    )
    return jax.shard_map(
        shards,
        mesh=mesh,
        in_specs=placed,
        out_specs=P(None, ("dp", "expert"), None),
        check_vma=False,
    )
```

```python
import functools

import jax
import jax.numpy as jnp
from jax import lax
from jax.experimental import pallas as pl
from jax.experimental.pallas import tpu as pltpu
from jax.sharding import PartitionSpec as P

HEAD_WIDTH = 128
CAP = 6
PACK = 8
SPLIT = CAP // (PACK - CAP)
GROUPS = 3
PERMUTED_WIDTH = 8
MIB = 1024 * 1024

F32 = jnp.float32
BF16 = jnp.bfloat16


def dot(a, b, dims=((1,), (0,))):
    return lax.dot_general(a, b, (dims, ((), ())), preferred_element_type=F32)


def row_iota(shape, axis):
    return lax.broadcasted_iota(jnp.int32, shape, axis)


def count_steps(value, step, upto):
    total = jnp.zeros_like(value)
    for at in range(1, upto):
        total = total + (value >= step * at).astype(jnp.int32)
    return total


def slot_picks(order, relative, holds_ref, dup_ref, routes_ref):
    _, batches, tokens = routes_ref.shape
    lanes = batches * tokens
    rows = len(order) * GROUPS * PACK
    shape = (rows, lanes)
    row = row_iota(shape, 0)
    lane = row_iota(shape, 1)
    block = count_steps(row, GROUPS * PACK, len(order))
    within = row - block * (GROUPS * PACK)
    group = count_steps(within, PACK, GROUPS)
    place = within - group * PACK
    me = lax.axis_index("expert") if relative else 0
    expert = jnp.zeros(shape, jnp.int32)
    for at, slot in enumerate(order):
        expert = jnp.where(block == at, holds_ref[me ^ slot], expert)
    doubled = jnp.zeros(shape, jnp.bool_)
    for at in range(dup_ref.shape[0]):
        doubled = doubled | (expert == dup_ref[at])
    batch = (lane >= tokens).astype(jnp.int32)
    allowed = (batch == (group >= 1).astype(jnp.int32)) & (doubled | (group < 2))
    routes = routes_ref[...]
    routes = jnp.concatenate([routes[:, at, :] for at in range(batches)], axis=1)
    named = [routes[k : k + 1, :] == expert for k in range(routes.shape[0])]
    hit = functools.reduce(jnp.logical_or, named)
    earlier = row_iota((lanes, lanes), 0)
    later = row_iota((lanes, lanes), 1)
    same = (earlier >= tokens) == (later >= tokens)
    before_mat = jnp.where((earlier < later) & same, 1.0, 0.0).astype(BF16)
    before = dot(jnp.where(hit, 1.0, 0.0).astype(BF16), before_mat).astype(jnp.int32)
    before = before - jnp.where(group == 2, CAP, 0)
    live = hit & allowed
    lead = live & (place < CAP) & (before == place)
    trail = [
        live & (place >= CAP) & (before == (place - CAP) * SPLIT + piece) for piece in range(SPLIT)
    ]
    return lead, trail, named


def attend(query_ref, key_ref, value_ref, lengths_ref, batch, attn_ref):
    tokens = query_ref.shape[1]
    kv_heads = key_ref.shape[2] // HEAD_WIDTH
    group = query_ref.shape[2] // HEAD_WIDTH // kv_heads
    at_row = row_iota((tokens, tokens), 0)
    at_col = row_iota((tokens, tokens), 1)
    row_request = jnp.zeros((tokens, tokens), jnp.int32)
    col_request = jnp.zeros((tokens, tokens), jnp.int32)
    end = jnp.int32(0)
    for r in range(lengths_ref.shape[2]):
        end = end + lengths_ref[batch, 0, r]
        row_request = row_request + (at_row >= end).astype(jnp.int32)
        col_request = col_request + (at_col >= end).astype(jnp.int32)
    allowed = (row_request == col_request) & (at_col <= at_row)
    squares = jnp.zeros((tokens, HEAD_WIDTH), F32)
    for h in range(kv_heads):
        kv = slice(h * HEAD_WIDTH, (h + 1) * HEAD_WIDTH)
        heads = [
            slice((h * group + g) * HEAD_WIDTH, (h * group + g + 1) * HEAD_WIDTH)
            for g in range(group)
        ]
        q = jnp.concatenate([query_ref[batch, :, cols] for cols in heads], axis=0)
        scores = dot(q, key_ref[batch, :, kv], ((1,), (1,))) * HEAD_WIDTH ** (-0.5)
        scores = scores.reshape(group, tokens, tokens)
        scores = jnp.where(allowed[None], scores, -1e30)
        weights = jnp.exp(scores - jnp.max(scores, axis=-1, keepdims=True))
        probs = (weights / jnp.sum(weights, axis=-1, keepdims=True)).astype(BF16)
        mixed = dot(probs.reshape(group * tokens, tokens), value_ref[batch, :, kv])
        for g, cols in enumerate(heads):
            part = mixed[g * tokens : (g + 1) * tokens]
            attn_ref[batch, :, cols] = part
            squares = squares + part * part
    meansq = jnp.sum(squares, axis=-1, keepdims=True) / query_ref.shape[2]
    return lax.rsqrt(meansq + 1e-05)


def front_kernel(
    order,
    relative,
    lengths_ref,
    holds_ref,
    dup_ref,
    query_ref,
    key_ref,
    value_ref,
    routes_ref,
    gain_ref,
    attn_ref,
    *rest,
):
    *send_refs, normed_ref = rest
    batches, tokens, features = query_ref.shape
    piece, cols = send_refs[0].shape
    step = cols // SPLIT
    for b in range(batches):
        scale = attend(query_ref, key_ref, value_ref, lengths_ref, b, attn_ref)
        normed_ref[b * tokens : (b + 1) * tokens, :] = (
            attn_ref[b] * scale * gain_ref[...]
        ).astype(BF16)
    lead, trail, _ = slot_picks(order, relative, holds_ref, dup_ref, routes_ref)
    tail = normed_ref[:, cols:features]
    for j in range(SPLIT):
        at = slice(j * step, (j + 1) * step)
        picks = jnp.concatenate([lead, trail[j]], axis=1)
        picks = jnp.where(picks, 1.0, 0.0).astype(BF16)
        source = jnp.concatenate([normed_ref[:, at], tail], axis=0)
        packed = dot(picks, source)
        for i, send_ref in enumerate(send_refs):
            send_ref[:, at] = packed[i * piece : (i + 1) * piece].astype(BF16)


def prepare_kernel(
    order,
    relative,
    holds_ref,
    dup_ref,
    routes_ref,
    gates_ref,
    gate_hbm,
    up_hbm,
    down_hbm,
    gate_ref,
    up_ref,
    down_ref,
    *rest,
):
    *mix_refs, sems = rest
    pairs = ((gate_hbm, gate_ref), (up_hbm, up_ref), (down_hbm, down_ref))
    loads = [pltpu.make_async_copy(a, b, sems.at[i]) for i, (a, b) in enumerate(pairs)]
    for load in loads:
        load.start()
    lead, trail, named = slot_picks(order, relative, holds_ref, dup_ref, routes_ref)
    gates = gates_ref[...]
    gates = jnp.concatenate([gates[:, at, :] for at in range(gates.shape[1])], axis=1)
    gate = jnp.zeros(lead.shape, F32)
    for k, match in enumerate(named):
        gate = gate + jnp.where(match, gates[k : k + 1, :], 0.0)
    lanes = lead.shape[1]
    rows = mix_refs[0].shape[2]
    for j in range(SPLIT):
        for part, pick in enumerate((lead, trail[j])):
            weight = jnp.where(pick, gate, 0.0)
            for i, mix_ref in enumerate(mix_refs):
                mine = weight[i * rows : (i + 1) * rows].T
                high = mine.astype(BF16)
                low = (mine - high.astype(F32)).astype(BF16)
                mix_ref[j, (2 * part) * lanes : (2 * part + 1) * lanes, :] = high
                mix_ref[j, (2 * part + 1) * lanes : (2 * part + 2) * lanes, :] = low
    for load in loads:
        load.wait()


def expert_kernel(count, gate_ref, up_ref, down_ref, *rest):
    got_refs, back_refs = rest[:count], rest[count : 2 * count]
    rows_ref, hidden_ref = rest[2 * count :]
    piece, cols = got_refs[0].shape
    features = rows_ref.shape[1]
    step = cols // SPLIT
    block, hidden = hidden_ref.shape
    shape = (block, block)
    row = row_iota(shape, 0)
    other = row_iota(shape, 1)
    place = lax.rem(row, PACK)
    tile = row - place

    def trails(j):
        picked = jnp.zeros(shape, jnp.bool_)
        for a in range(PACK - CAP):
            picked = picked | ((place == a * SPLIT + j) & (other == tile + CAP + a))
        return jnp.where(picked, 1.0, 0.0).astype(BF16)

    take = min(piece, block)
    for start in range(0, piece * count, block):
        spots = [
            (at // piece, slice(at % piece, at % piece + take), slice(at - start, at - start + take))
            for at in range(start, start + block, take)
        ]
        for i, theirs, mine in spots:
            rows_ref[mine, :cols] = got_refs[i][theirs, :]
        tail = jnp.zeros((block, features - cols), F32)
        for j in range(SPLIT):
            tail = tail + dot(trails(j), rows_ref[:, j * step : (j + 1) * step])
        rows_ref[:, cols:] = tail.astype(BF16)
        chunk = 256 if hidden % 256 == 0 else hidden
        for c in range(0, hidden, chunk):
            gate_val = dot(rows_ref[...], gate_ref[0, :, c : c + chunk])
            up_val = dot(rows_ref[...], up_ref[0, :, c : c + chunk])
            hidden_ref[:, c : c + chunk] = (
                gate_val / (1.0 + jnp.exp(-gate_val)) * up_val
            ).astype(BF16)
        tail = dot(hidden_ref[...], down_ref[0, :, cols:]).astype(BF16)
        leading = lax.rem(row_iota((block, step), 0), PACK) < CAP
        for j in range(SPLIT):
            at = slice(j * step, (j + 1) * step)
            moved = dot(trails(j), tail, ((0,), (0,)))
            result = jnp.where(leading, dot(hidden_ref[...], down_ref[0, :, at]), moved)
            for i, theirs, mine in spots:
                back_refs[i][theirs, at] = result[mine].astype(BF16)


def combine_kernel(base_ref, mix_ref, *rest):
    *back_refs, out_ref = rest
    batches, tokens, features = base_ref.shape
    lanes = batches * tokens
    piece, cols = back_refs[0].shape
    step = cols // SPLIT
    tail = jnp.zeros((lanes, features - cols), F32)

    def put(part, at):
        for b in range(batches):
            out_ref[b, :, at] = (base_ref[b, :, at] + part[b * tokens : (b + 1) * tokens]).astype(
                out_ref.dtype
            )

    for j in range(SPLIT):
        at = slice(j * step, (j + 1) * step)
        back = jnp.concatenate([back_ref[:, at] for back_ref in back_refs], axis=0)
        mixed = dot(mix_ref[j], back)
        put(mixed[:lanes] + mixed[lanes : 2 * lanes], at)
        tail = tail + (mixed[2 * lanes : 3 * lanes] + mixed[3 * lanes :])
    put(tail, slice(cols, features))


def results(in_vmem, *shapes):
    kind = pltpu.VMEM if in_vmem else jax.ShapeDtypeStruct
    return [kind(shape, dtype) for shape, dtype in shapes]


def from_hbm(*values):
    return [pltpu.with_memory_space_constraint(value, pltpu.HBM) for value in values]


def in_vmem(count):
    return [pl.BlockSpec(memory_space=pltpu.VMEM)] * count


def in_smem(count):
    return [pl.BlockSpec(memory_space=pltpu.SMEM)] * count


def peer_groups(width):
    half = width // 2
    far, near = list(range(half, width)), [1, 0] + list(range(2, half))
    return [far[: half // 2] + near[: half // 2], far[half // 2 :] + near[half // 2 :]]


def swap(value, peer):
    if peer == 0:
        return value
    pairs = [(source, source ^ peer) for source in range(lax.axis_size("expert"))]
    return lax.ppermute(value, "expert", pairs)


def exchange_all(value):
    return lax.all_to_all(value, "expert", split_axis=0, concat_axis=0, tiled=True)


def shards(
    query,
    keys,
    values,
    lengths,
    routes,
    gates,
    norm_gain,
    old_holds,
    dup_experts,
    w_gate,
    w_up,
    w_down,
):
    width = lax.axis_size("expert")
    batches, tokens, features = query.shape
    lanes = batches * tokens
    cols = features * CAP // PACK
    hidden = w_gate.shape[2]
    relative = width == PERMUTED_WIDTH
    groups = peer_groups(width) if relative else [list(range(width))]
    order = [peer for group in groups for peer in group]
    block = GROUPS * PACK
    piece = block if relative else block * width
    counts = [len(group) * block // piece for group in groups]
    params = pltpu.CompilerParams(vmem_limit_bytes=24 * MIB if relative else 56 * MIB)
    routes = jnp.transpose(routes, (2, 0, 1))
    gates = jnp.transpose(gates, (2, 0, 1))
    gain = norm_gain.reshape(1, features)

    attn, *send = pl.pallas_call(
        functools.partial(front_kernel, order, relative),
        name="attend_and_pack",
        out_shape=results(
            relative, ((batches, tokens, features), F32), *[((piece, cols), BF16)] * sum(counts)
        ),
        in_specs=in_smem(3) + in_vmem(5),
        out_specs=in_vmem(1 + sum(counts)),
        scratch_shapes=[pltpu.VMEM((lanes, features), BF16)],
        compiler_params=params,
    )(*from_hbm(lengths, old_holds, dup_experts, query, keys, values, routes, gain))

    def travel(parts, group):
        if relative:
            return [swap(part, peer) for part, peer in zip(parts, group)]
        return [exchange_all(part) for part in parts]

    arrived, at = [], 0
    for group, count in zip(groups, counts):
        arrived.append(travel(send[at : at + count], group))
        at += count

    big = [w_gate, w_up, w_down]
    gate_mat, up_mat, down_mat, *mixes = pl.pallas_call(
        functools.partial(prepare_kernel, order, relative),
        name="prepare",
        out_shape=results(
            relative,
            *[(w.shape, w.dtype) for w in big],
            *[((SPLIT, 4 * lanes, len(group) * block), BF16) for group in groups],
        ),
        in_specs=in_smem(2) + in_vmem(2) + [pl.BlockSpec(memory_space=pltpu.HBM)] * 3,
        out_specs=in_vmem(3 + len(groups)),
        scratch_shapes=[pltpu.SemaphoreType.DMA((3,))],
        cost_estimate=pl.CostEstimate(
            flops=0, bytes_accessed=sum(2 * w.size * 2 for w in big), transcendentals=0
        ),
        compiler_params=params,
    )(*from_hbm(old_holds, dup_experts, routes, gates, *big))

    returned = []
    for group, count, got in zip(groups, counts, arrived):
        rows = min(count * piece, block * 8)
        back = pl.pallas_call(
            functools.partial(expert_kernel, count),
            name="expert_ffn",
            out_shape=[jax.ShapeDtypeStruct((piece, cols), BF16)] * count,
            in_specs=in_vmem(3 + count),
            out_specs=in_vmem(count),
            scratch_shapes=[pltpu.VMEM((rows, features), BF16), pltpu.VMEM((rows, hidden), BF16)],
            cost_estimate=pl.CostEstimate(
                flops=count * piece * features * hidden * 6,
                bytes_accessed=sum(w.size * 2 for w in big),
                transcendentals=0,
            ),
            compiler_params=params,
        )(gate_mat, up_mat, down_mat, *got)
        returned.append(travel(back, group))

    base = attn
    for at, (mix, back) in enumerate(zip(mixes, returned)):
        last = at == len(groups) - 1
        base = pl.pallas_call(
            combine_kernel,
            name="combine",
            out_shape=jax.ShapeDtypeStruct(attn.shape, BF16 if last else F32),
            in_specs=in_vmem(2 + len(back)),
            out_specs=in_vmem(1)[0],
            cost_estimate=pl.CostEstimate(
                flops=2 * mix.size * features // SPLIT,
                bytes_accessed=attn.size * 8,
                transcendentals=0,
            ),
            compiler_params=params,
        )(base, mix, *back)
    return base


def solution(mesh):
    placed = (
        P(None, ("dp", "expert"), None),
        P(None, ("dp", "expert"), None),
        P(None, ("dp", "expert"), None),
        P(None, ("dp", "expert"), None),
        P(None, ("dp", "expert"), None),
        P(None, ("dp", "expert"), None),
        P(),
        P(),
        P(),
        P("expert", None, None),
        P("expert", None, None),
        P("expert", None, None),
    )
    return jax.shard_map(
        shards,
        mesh=mesh,
        in_specs=placed,
        out_specs=P(None, ("dp", "expert"), None),
        check_vma=False,
    )
```

```python
import functools
import math

import jax
import jax.numpy as jnp
from jax import lax
from jax.experimental import pallas as pl
from jax.experimental.pallas import tpu as pltpu
from jax.sharding import PartitionSpec as P

HEAD_WIDTH = 128
CAP = 6
PACK = 8
SPLIT = CAP // (PACK - CAP)
GROUPS = 3
PERMUTED_WIDTH = 8
MIB = 1024 * 1024

F32 = jnp.float32
BF16 = jnp.bfloat16


def dot(a, b, dims=((1,), (0,))):
    return lax.dot_general(a, b, (dims, ((), ())), preferred_element_type=F32)


def row_iota(shape, axis):
    return lax.broadcasted_iota(jnp.int32, shape, axis)


def count_steps(value, step, upto):
    total = jnp.zeros_like(value)
    for at in range(1, upto):
        total = total + (value >= step * at).astype(jnp.int32)
    return total


def slot_picks(order, relative, holds_ref, dup_ref, routes_ref):
    _, batches, tokens = routes_ref.shape
    lanes = batches * tokens
    shape = (len(order), lanes)
    block = row_iota(shape, 0)
    me = lax.axis_index("expert") if relative else 0
    expert = jnp.zeros(shape, jnp.int32)
    for at, slot in enumerate(order):
        expert = jnp.where(block == at, holds_ref[me ^ slot], expert)
    limit = jnp.full(shape, CAP, jnp.int32)
    for at in range(dup_ref.shape[0]):
        limit = jnp.where(expert == dup_ref[at], 2 * CAP, limit)
    limit = jnp.where(row_iota(shape, 1) >= tokens, limit, CAP)
    routes = routes_ref[...]
    routes = jnp.concatenate([routes[:, at, :] for at in range(batches)], axis=1)
    named = [routes[k : k + 1, :] == expert for k in range(routes.shape[0])]
    hit = functools.reduce(jnp.logical_or, named)
    earlier = row_iota((lanes, lanes), 0)
    later = row_iota((lanes, lanes), 1)
    same = (earlier >= tokens) == (later >= tokens)
    before_mat = jnp.where((earlier < later) & same, 1.0, 0.0).astype(BF16)
    before = dot(jnp.where(hit, 1.0, 0.0).astype(BF16), before_mat).astype(jnp.int32)
    before = jnp.where(hit & (before < limit), before, -1)

    shape = (GROUPS * PACK, lanes)
    row = row_iota(shape, 0)
    group = count_steps(row, PACK, GROUPS)
    place = row - group * PACK
    mine = (row_iota(shape, 1) >= tokens) == (group >= 1)
    first = jnp.where(group == 2, CAP, 0)
    lead_place = jnp.where(mine & (place < CAP), place + first, -2)
    trail_places = [
        jnp.where(mine & (place >= CAP), (place - CAP) * SPLIT + piece + first, -2)
        for piece in range(SPLIT)
    ]

    def matches(places):
        blocks = [
            jnp.where(before[at : at + 1, :] == places, 1.0, 0.0) for at in range(len(order))
        ]
        return jnp.concatenate(blocks, axis=0)

    return matches(lead_place), [matches(places) for places in trail_places], named


def attend(query_ref, key_ref, value_ref, lengths_ref, batch, attn_ref):
    tokens = query_ref.shape[1]
    kv_heads = key_ref.shape[2] // HEAD_WIDTH
    group = query_ref.shape[2] // HEAD_WIDTH // kv_heads
    at_row = row_iota((tokens, tokens), 0)
    at_col = row_iota((tokens, tokens), 1)
    row_request = jnp.zeros((tokens, tokens), jnp.int32)
    col_request = jnp.zeros((tokens, tokens), jnp.int32)
    end = jnp.int32(0)
    for r in range(lengths_ref.shape[2]):
        end = end + lengths_ref[batch, 0, r]
        row_request = row_request + (at_row >= end).astype(jnp.int32)
        col_request = col_request + (at_col >= end).astype(jnp.int32)
    allowed = (row_request == col_request) & (at_col <= at_row)
    bias = jnp.where(allowed, 0.0, -1e30)
    scale = HEAD_WIDTH ** (-0.5) * math.log2(math.e)
    squares = jnp.zeros((tokens, HEAD_WIDTH), F32)
    for h in range(kv_heads):
        kv = slice(h * HEAD_WIDTH, (h + 1) * HEAD_WIDTH)
        heads = [
            slice((h * group + g) * HEAD_WIDTH, (h * group + g + 1) * HEAD_WIDTH)
            for g in range(group)
        ]
        q = jnp.concatenate([query_ref[batch, :, cols] for cols in heads], axis=0)
        scores = dot(q, key_ref[batch, :, kv], ((1,), (1,)))
        scores = scores.reshape(group, tokens, tokens) + bias[None]
        weights = jnp.exp2((scores - jnp.max(scores, axis=-1, keepdims=True)) * scale)
        share = 1.0 / jnp.sum(weights, axis=-1, keepdims=True)
        probs = (weights * share).astype(BF16)
        mixed = dot(probs.reshape(group * tokens, tokens), value_ref[batch, :, kv])
        for g, cols in enumerate(heads):
            part = mixed[g * tokens : (g + 1) * tokens]
            attn_ref[batch, :, cols] = part
            squares = squares + part * part
    meansq = jnp.sum(squares, axis=-1, keepdims=True) / query_ref.shape[2]
    return lax.rsqrt(meansq + 1e-05)


def front_kernel(
    order,
    relative,
    lengths_ref,
    holds_ref,
    dup_ref,
    query_ref,
    key_ref,
    value_ref,
    routes_ref,
    gain_ref,
    attn_ref,
    *rest,
):
    *send_refs, normed_ref = rest
    batches, tokens, features = query_ref.shape
    piece, cols = send_refs[0].shape
    step = cols // SPLIT
    for b in range(batches):
        scale = attend(query_ref, key_ref, value_ref, lengths_ref, b, attn_ref)
        normed_ref[b * tokens : (b + 1) * tokens, :] = (
            attn_ref[b] * scale * gain_ref[...][None, :]
        ).astype(BF16)
    lead, trail, _ = slot_picks(order, relative, holds_ref, dup_ref, routes_ref)
    tail = normed_ref[:, cols:features]
    for j in range(SPLIT):
        at = slice(j * step, (j + 1) * step)
        picks = jnp.concatenate([lead, trail[j]], axis=1).astype(BF16)
        source = jnp.concatenate([normed_ref[:, at], tail], axis=0)
        packed = dot(picks, source)
        for i, send_ref in enumerate(send_refs):
            send_ref[:, at] = packed[i * piece : (i + 1) * piece].astype(BF16)


def load_kernel(*refs):
    *refs, sems = refs
    half = len(refs) // 2
    loads = [
        pltpu.make_async_copy(refs[i], refs[half + i], sems.at[i]) for i in range(half)
    ]
    for load in loads:
        load.start()
    for load in loads:
        load.wait()


def weights_kernel(order, relative, holds_ref, dup_ref, routes_ref, gates_ref, *mix_refs):
    lead, trail, named = slot_picks(order, relative, holds_ref, dup_ref, routes_ref)
    gates = gates_ref[...]
    gates = jnp.concatenate([gates[:, at, :] for at in range(gates.shape[1])], axis=1)
    gate = jnp.zeros(named[0].shape, F32)
    for k, match in enumerate(named):
        gate = gate + jnp.where(match, gates[k : k + 1, :], 0.0)
    high = gate.astype(BF16).astype(F32)
    lanes = lead.shape[1]
    rows = mix_refs[0].shape[2] // 2
    block = GROUPS * PACK
    for k, part in enumerate((high, gate - high)):
        spread = [jnp.broadcast_to(part[at : at + 1], (block, lanes)) for at in range(len(order))]
        spread = jnp.concatenate(spread, axis=0)
        for j in range(SPLIT):
            for half, pick in enumerate((lead, trail[j])):
                weight = pick * spread
                for i, mix_ref in enumerate(mix_refs):
                    mix_ref[j, half * lanes : (half + 1) * lanes, k * rows : (k + 1) * rows] = (
                        weight[i * rows : (i + 1) * rows].T.astype(BF16)
                    )


def expert_kernel(count, gate_ref, up_ref, down_ref, *rest):
    got_refs, back_refs = rest[:count], rest[count : 2 * count]
    rows_ref, hidden_ref = rest[2 * count :]
    piece, cols = got_refs[0].shape
    features = rows_ref.shape[1]
    step = cols // SPLIT
    block, hidden = hidden_ref.shape
    shape = (block, block)
    row = row_iota(shape, 0)
    other = row_iota(shape, 1)
    place = lax.rem(row, PACK)
    tile = row - place

    def trails(j):
        picked = jnp.zeros(shape, jnp.bool_)
        for a in range(PACK - CAP):
            picked = picked | ((place == a * SPLIT + j) & (other == tile + CAP + a))
        return jnp.where(picked, 1.0, 0.0).astype(BF16)

    take = min(piece, block)
    for start in range(0, piece * count, block):
        spots = [
            (at // piece, slice(at % piece, at % piece + take), slice(at - start, at - start + take))
            for at in range(start, start + block, take)
        ]
        for i, theirs, mine in spots:
            rows_ref[mine, :cols] = got_refs[i][theirs, :]
        tail = jnp.zeros((block, features - cols), F32)
        for j in range(SPLIT):
            tail = tail + dot(trails(j), rows_ref[:, j * step : (j + 1) * step])
        rows_ref[:, cols:] = tail.astype(BF16)
        chunk = 256 if hidden % 256 == 0 else hidden
        for c in range(0, hidden, chunk):
            gate_val = dot(rows_ref[...], gate_ref[0, :, c : c + chunk])
            up_val = dot(rows_ref[...], up_ref[0, :, c : c + chunk])
            hidden_ref[:, c : c + chunk] = (
                gate_val / (1.0 + jnp.exp(-gate_val)) * up_val
            ).astype(BF16)
        tail = dot(hidden_ref[...], down_ref[0, :, cols:]).astype(BF16)
        leading = lax.rem(row_iota((block, step), 0), PACK) < CAP
        for j in range(SPLIT):
            at = slice(j * step, (j + 1) * step)
            moved = dot(trails(j), tail, ((0,), (0,)))
            result = jnp.where(leading, dot(hidden_ref[...], down_ref[0, :, at]), moved)
            for i, theirs, mine in spots:
                back_refs[i][theirs, at] = result[mine].astype(BF16)


def combine_kernel(base_ref, mix_ref, *rest):
    *back_refs, out_ref = rest
    batches, tokens, features = base_ref.shape
    lanes = batches * tokens
    piece, cols = back_refs[0].shape
    step = cols // SPLIT
    tail = jnp.zeros((lanes, features - cols), F32)

    def put(part, at):
        for b in range(batches):
            out_ref[b, :, at] = (base_ref[b, :, at] + part[b * tokens : (b + 1) * tokens]).astype(
                out_ref.dtype
            )

    for j in range(SPLIT):
        at = slice(j * step, (j + 1) * step)
        back = jnp.concatenate([back_ref[:, at] for back_ref in back_refs] * 2, axis=0)
        mixed = dot(mix_ref[j], back)
        put(mixed[:lanes], at)
        tail = tail + mixed[lanes:]
    put(tail, slice(cols, features))


def results(in_vmem, *shapes):
    kind = pltpu.VMEM if in_vmem else jax.ShapeDtypeStruct
    return [kind(shape, dtype) for shape, dtype in shapes]


def from_hbm(*values):
    return [pltpu.with_memory_space_constraint(value, pltpu.HBM) for value in values]


def in_vmem(count):
    return [pl.BlockSpec(memory_space=pltpu.VMEM)] * count


def in_smem(count):
    return [pl.BlockSpec(memory_space=pltpu.SMEM)] * count


def peer_groups(width):
    half = width // 2
    far, near = list(range(half, width)), [1, 0] + list(range(2, half))
    return [far[: half // 2] + near[: half // 2], far[half // 2 :] + near[half // 2 :]]


def swap(value, peer):
    if peer == 0:
        return value
    pairs = [(source, source ^ peer) for source in range(lax.axis_size("expert"))]
    return lax.ppermute(value, "expert", pairs)


def after(value, first):
    return lax.optimization_barrier((value, first))[0]


def load_weights(params, *weights):
    return pl.pallas_call(
        load_kernel,
        name="load_weights",
        out_shape=results(True, *[(w.shape, w.dtype) for w in weights]),
        in_specs=[pl.BlockSpec(memory_space=pltpu.HBM)] * len(weights),
        out_specs=in_vmem(len(weights)),
        scratch_shapes=[pltpu.SemaphoreType.DMA((len(weights),))],
        cost_estimate=pl.CostEstimate(
            flops=0, bytes_accessed=sum(w.size * 4 for w in weights), transcendentals=0
        ),
        compiler_params=params,
    )(*from_hbm(*weights))


def exchange_all(value):
    return lax.all_to_all(value, "expert", split_axis=0, concat_axis=0, tiled=True)


def shards(
    query,
    keys,
    values,
    lengths,
    routes,
    gates,
    norm_gain,
    old_holds,
    dup_experts,
    w_gate,
    w_up,
    w_down,
):
    width = lax.axis_size("expert")
    batches, tokens, features = query.shape
    lanes = batches * tokens
    cols = features * CAP // PACK
    hidden = w_gate.shape[2]
    relative = width == PERMUTED_WIDTH
    groups = peer_groups(width) if relative else [list(range(width))]
    order = [peer for group in groups for peer in group]
    block = GROUPS * PACK
    piece = block if relative else block * width
    counts = [len(group) * block // piece for group in groups]
    params = pltpu.CompilerParams(vmem_limit_bytes=24 * MIB if relative else 56 * MIB)
    routes = jnp.transpose(routes, (2, 0, 1))
    gates = jnp.transpose(gates, (2, 0, 1))

    attn, *send = pl.pallas_call(
        functools.partial(front_kernel, order, relative),
        name="attend_and_pack",
        out_shape=results(
            relative, ((batches, tokens, features), F32), *[((piece, cols), BF16)] * sum(counts)
        ),
        in_specs=in_smem(3) + in_vmem(5),
        out_specs=in_vmem(1 + sum(counts)),
        scratch_shapes=[pltpu.VMEM((lanes, features), BF16)],
        compiler_params=params,
    )(*from_hbm(lengths, old_holds, dup_experts, query, keys, values, routes, norm_gain))

    sent = dict(zip(order, send))
    arrived = {}
    gate_mat, up_mat, down_mat = w_gate, w_up, w_down
    if relative:
        half = width // 2
        for peer in groups[0]:
            arrived[peer] = swap(sent[peer], peer)
        gate_mat, up_mat = load_weights(params, w_gate, w_up)
        for peer in groups[1]:
            if peer >= half:
                arrived[peer] = swap(after(sent[peer], up_mat), peer)
        (down_mat,) = load_weights(params, after(w_down, up_mat))
        for peer in groups[1]:
            if peer < half:
                arrived[peer] = swap(after(sent[peer], down_mat), peer)
    else:
        arrived[0] = exchange_all(send[0])

    returned = []
    for group, count in zip(groups, counts):
        got = [arrived[peer] for peer in group[:count]]
        rows = min(count * piece, block * 8)
        back = pl.pallas_call(
            functools.partial(expert_kernel, count),
            name="expert_ffn",
            out_shape=results(relative, *[((piece, cols), BF16)] * count),
            in_specs=in_vmem(3 + count),
            out_specs=in_vmem(count),
            scratch_shapes=[pltpu.VMEM((rows, features), BF16), pltpu.VMEM((rows, hidden), BF16)],
            cost_estimate=pl.CostEstimate(
                flops=count * piece * features * hidden * 6,
                bytes_accessed=w_gate.size * 6,
                transcendentals=0,
            ),
            compiler_params=params,
        )(gate_mat, up_mat, down_mat, *got)
        if relative:
            returned.append([swap(part, peer) for part, peer in zip(back, group)])
        else:
            returned.append([exchange_all(part) for part in back])

    mixes = pl.pallas_call(
        functools.partial(weights_kernel, order, relative),
        name="gate_weights",
        out_shape=results(
            relative,
            *[((SPLIT, 2 * lanes, 2 * len(group) * block), BF16) for group in groups],
        ),
        in_specs=in_smem(2) + in_vmem(2),
        out_specs=in_vmem(len(groups)),
        cost_estimate=pl.CostEstimate(flops=0, bytes_accessed=4 * MIB, transcendentals=0),
        compiler_params=params,
    )(*from_hbm(old_holds, dup_experts, after(routes, back[0]), gates))

    base = attn
    for at, (mix, back) in enumerate(zip(mixes, returned)):
        last = at == len(groups) - 1
        base = pl.pallas_call(
            combine_kernel,
            name="combine",
            out_shape=jax.ShapeDtypeStruct(attn.shape, BF16 if last else F32),
            in_specs=in_vmem(2 + len(back)),
            out_specs=in_vmem(1)[0],
            cost_estimate=pl.CostEstimate(
                flops=2 * mix.size * features // SPLIT,
                bytes_accessed=attn.size * 8,
                transcendentals=0,
            ),
            compiler_params=params,
        )(base, mix, *back)
    return base


def solution(mesh):
    placed = (
        P(None, ("dp", "expert"), None),
        P(None, ("dp", "expert"), None),
        P(None, ("dp", "expert"), None),
        P(None, ("dp", "expert"), None),
        P(None, ("dp", "expert"), None),
        P(None, ("dp", "expert"), None),
        P(),
        P(),
        P(),
        P("expert", None, None),
        P("expert", None, None),
        P("expert", None, None),
    )
    return jax.shard_map(
        shards,
        mesh=mesh,
        in_specs=placed,
        out_specs=P(None, ("dp", "expert"), None),
        check_vma=False,
    )
```

```python
import functools
import math

import jax
import jax.numpy as jnp
from jax import lax
from jax.experimental import pallas as pl
from jax.experimental.pallas import tpu as pltpu
from jax.sharding import PartitionSpec as P

HEAD_WIDTH = 128
CAP = 6
PACK = 8
SPLIT = CAP // (PACK - CAP)
GROUPS = 3
PERMUTED_WIDTH = 8
PEER_GROUPS = [[4, 7, 1, 0], [5, 6, 2, 3]]
MIB = 1024 * 1024

F32 = jnp.float32
BF16 = jnp.bfloat16


def dot(a, b, dims=((1,), (0,))):
    return lax.dot_general(a, b, (dims, ((), ())), preferred_element_type=F32)


def row_iota(shape, axis):
    return lax.broadcasted_iota(jnp.int32, shape, axis)


def count_steps(value, step, upto):
    total = jnp.zeros_like(value)
    for at in range(1, upto):
        total = total + (value >= step * at).astype(jnp.int32)
    return total


def slot_picks(order, relative, holds_ref, dup_ref, routes_ref):
    _, batches, tokens = routes_ref.shape
    lanes = batches * tokens
    shape = (len(order), lanes)
    block = row_iota(shape, 0)
    me = lax.axis_index("expert") if relative else 0
    expert = jnp.zeros(shape, jnp.int32)
    for at, slot in enumerate(order):
        expert = jnp.where(block == at, holds_ref[me ^ slot], expert)
    limit = jnp.full(shape, CAP, jnp.int32)
    for at in range(dup_ref.shape[0]):
        limit = jnp.where(expert == dup_ref[at], 2 * CAP, limit)
    limit = jnp.where(row_iota(shape, 1) >= tokens, limit, CAP)
    routes = routes_ref[...]
    routes = jnp.concatenate([routes[:, at, :] for at in range(batches)], axis=1)
    named = [routes[k : k + 1, :] == expert for k in range(routes.shape[0])]
    hit = functools.reduce(jnp.logical_or, named)
    earlier = row_iota((lanes, lanes), 0)
    later = row_iota((lanes, lanes), 1)
    same = (earlier >= tokens) == (later >= tokens)
    before_mat = jnp.where((earlier < later) & same, 1.0, 0.0).astype(BF16)
    before = dot(jnp.where(hit, 1.0, 0.0).astype(BF16), before_mat).astype(jnp.int32)
    before = jnp.where(hit & (before < limit), before, -1)

    shape = (GROUPS * PACK, lanes)
    row = row_iota(shape, 0)
    group = count_steps(row, PACK, GROUPS)
    place = row - group * PACK
    mine = (row_iota(shape, 1) >= tokens) == (group >= 1)
    first = jnp.where(group == 2, CAP, 0)
    lead_place = jnp.where(mine & (place < CAP), place + first, -2)
    trail_places = [
        jnp.where(mine & (place >= CAP), (place - CAP) * SPLIT + piece + first, -2)
        for piece in range(SPLIT)
    ]

    def matches(places):
        blocks = [
            jnp.where(before[at : at + 1, :] == places, 1.0, 0.0) for at in range(len(order))
        ]
        return jnp.concatenate(blocks, axis=0)

    return matches(lead_place), [matches(places) for places in trail_places], named


def attend(query_ref, key_ref, value_ref, lengths_ref, batch, attn_ref):
    tokens = query_ref.shape[1]
    kv_heads = key_ref.shape[2] // HEAD_WIDTH
    group = query_ref.shape[2] // HEAD_WIDTH // kv_heads
    at_row = row_iota((tokens, tokens), 0)
    at_col = row_iota((tokens, tokens), 1)
    row_request = jnp.zeros((tokens, tokens), jnp.int32)
    col_request = jnp.zeros((tokens, tokens), jnp.int32)
    end = jnp.int32(0)
    for r in range(lengths_ref.shape[2]):
        end = end + lengths_ref[batch, 0, r]
        row_request = row_request + (at_row >= end).astype(jnp.int32)
        col_request = col_request + (at_col >= end).astype(jnp.int32)
    allowed = (row_request == col_request) & (at_col <= at_row)
    bias = jnp.where(allowed, 0.0, -1e30)
    scale = HEAD_WIDTH ** (-0.5) * math.log2(math.e)
    squares = jnp.zeros((tokens, HEAD_WIDTH), F32)
    for h in range(kv_heads):
        kv = slice(h * HEAD_WIDTH, (h + 1) * HEAD_WIDTH)
        heads = [
            slice((h * group + g) * HEAD_WIDTH, (h * group + g + 1) * HEAD_WIDTH)
            for g in range(group)
        ]
        q = jnp.concatenate([query_ref[batch, :, cols] for cols in heads], axis=0)
        scores = dot(q, key_ref[batch, :, kv], ((1,), (1,)))
        scores = scores.reshape(group, tokens, tokens) + bias[None]
        weights = jnp.exp2((scores - jnp.max(scores, axis=-1, keepdims=True)) * scale)
        share = 1.0 / jnp.sum(weights, axis=-1, keepdims=True)
        probs = (weights * share).astype(BF16)
        mixed = dot(probs.reshape(group * tokens, tokens), value_ref[batch, :, kv])
        for g, cols in enumerate(heads):
            part = mixed[g * tokens : (g + 1) * tokens]
            attn_ref[batch, :, cols] = part
            squares = squares + part * part
    meansq = jnp.sum(squares, axis=-1, keepdims=True) / query_ref.shape[2]
    return lax.rsqrt(meansq + 1e-05)


def front_kernel(
    order,
    relative,
    lengths_ref,
    holds_ref,
    dup_ref,
    query_ref,
    key_ref,
    value_ref,
    routes_ref,
    gain_ref,
    *rest,
):
    if relative:
        gate_hbm, gate_ref, attn_ref, *send_refs, normed_ref, sem = rest
        load = pltpu.make_async_copy(gate_hbm, gate_ref, sem)
        load.start()
    else:
        attn_ref, *send_refs, normed_ref = rest
    batches, tokens, features = query_ref.shape
    piece, cols = send_refs[0].shape
    step = cols // SPLIT

    @pl.when(holds_ref[0] >= 0)
    def _():
        for b in range(batches):
            scale = attend(query_ref, key_ref, value_ref, lengths_ref, b, attn_ref)
            normed_ref[b * tokens : (b + 1) * tokens, :] = (
                attn_ref[b] * scale * gain_ref[...][None, :]
            ).astype(BF16)
        lead, trail, _ = slot_picks(order, relative, holds_ref, dup_ref, routes_ref)
        tail = normed_ref[:, cols:features]
        for j in range(SPLIT):
            at = slice(j * step, (j + 1) * step)
            picks = jnp.concatenate([lead, trail[j]], axis=1).astype(BF16)
            source = jnp.concatenate([normed_ref[:, at], tail], axis=0)
            packed = dot(picks, source)
            for i, send_ref in enumerate(send_refs):
                send_ref[:, at] = packed[i * piece : (i + 1) * piece].astype(BF16)

    if relative:
        load.wait()


def load_kernel(*refs):
    *refs, sems = refs
    half = len(refs) // 2
    loads = [
        pltpu.make_async_copy(refs[i], refs[half + i], sems.at[i]) for i in range(half)
    ]
    for load in loads:
        load.start()
    for load in loads:
        load.wait()


def weights_kernel(order, relative, holds_ref, dup_ref, routes_ref, gates_ref, *mix_refs):
    lead, trail, named = slot_picks(order, relative, holds_ref, dup_ref, routes_ref)
    gates = gates_ref[...]
    gates = jnp.concatenate([gates[:, at, :] for at in range(gates.shape[1])], axis=1)
    gate = jnp.zeros(named[0].shape, F32)
    for k, match in enumerate(named):
        gate = gate + jnp.where(match, gates[k : k + 1, :], 0.0)
    high = gate.astype(BF16).astype(F32)
    lanes = lead.shape[1]
    rows = mix_refs[0].shape[2] // 2
    block = GROUPS * PACK
    for k, part in enumerate((high, gate - high)):
        spread = [jnp.broadcast_to(part[at : at + 1], (block, lanes)) for at in range(len(order))]
        spread = jnp.concatenate(spread, axis=0)
        for j in range(SPLIT):
            for half, pick in enumerate((lead, trail[j])):
                weight = pick * spread
                for i, mix_ref in enumerate(mix_refs):
                    mix_ref[j, half * lanes : (half + 1) * lanes, k * rows : (k + 1) * rows] = (
                        weight[i * rows : (i + 1) * rows].T.astype(BF16)
                    )


def expert_kernel(count, gate_ref, up_ref, down_ref, *rest):
    got_refs, back_refs = rest[:count], rest[count : 2 * count]
    rows_ref, hidden_ref = rest[2 * count :]
    piece, cols = got_refs[0].shape
    features = rows_ref.shape[1]
    step = cols // SPLIT
    block, hidden = hidden_ref.shape
    shape = (block, block)
    row = row_iota(shape, 0)
    other = row_iota(shape, 1)
    place = lax.rem(row, PACK)
    tile = row - place

    def trails(j):
        picked = jnp.zeros(shape, jnp.bool_)
        for a in range(PACK - CAP):
            picked = picked | ((place == a * SPLIT + j) & (other == tile + CAP + a))
        return jnp.where(picked, 1.0, 0.0).astype(BF16)

    take = min(piece, block)
    for start in range(0, piece * count, block):
        spots = [
            (at // piece, slice(at % piece, at % piece + take), slice(at - start, at - start + take))
            for at in range(start, start + block, take)
        ]
        for i, theirs, mine in spots:
            rows_ref[mine, :cols] = got_refs[i][theirs, :]
        tail = jnp.zeros((block, features - cols), F32)
        for j in range(SPLIT):
            tail = tail + dot(trails(j), rows_ref[:, j * step : (j + 1) * step])
        rows_ref[:, cols:] = tail.astype(BF16)
        chunk = 256 if hidden % 256 == 0 else hidden
        for c in range(0, hidden, chunk):
            gate_val = dot(rows_ref[...], gate_ref[0, :, c : c + chunk])
            up_val = dot(rows_ref[...], up_ref[0, :, c : c + chunk])
            hidden_ref[:, c : c + chunk] = (
                gate_val / (1.0 + jnp.exp(-gate_val)) * up_val
            ).astype(BF16)
        tail = dot(hidden_ref[...], down_ref[0, :, cols:]).astype(BF16)
        leading = lax.rem(row_iota((block, step), 0), PACK) < CAP
        for j in range(SPLIT):
            at = slice(j * step, (j + 1) * step)
            moved = dot(trails(j), tail, ((0,), (0,)))
            result = jnp.where(leading, dot(hidden_ref[...], down_ref[0, :, at]), moved)
            for i, theirs, mine in spots:
                back_refs[i][theirs, at] = result[mine].astype(BF16)


def combine_kernel(base_ref, mix_ref, *rest):
    *back_refs, out_ref = rest
    batches, tokens, features = base_ref.shape
    lanes = batches * tokens
    piece, cols = back_refs[0].shape
    step = cols // SPLIT
    tail = jnp.zeros((lanes, features - cols), F32)

    def put(part, at):
        for b in range(batches):
            out_ref[b, :, at] = (base_ref[b, :, at] + part[b * tokens : (b + 1) * tokens]).astype(
                out_ref.dtype
            )

    for j in range(SPLIT):
        at = slice(j * step, (j + 1) * step)
        back = jnp.concatenate([back_ref[:, at] for back_ref in back_refs] * 2, axis=0)
        mixed = dot(mix_ref[j], back)
        put(mixed[:lanes], at)
        tail = tail + mixed[lanes:]
    put(tail, slice(cols, features))


def results(in_vmem, *shapes):
    kind = pltpu.VMEM if in_vmem else jax.ShapeDtypeStruct
    return [kind(shape, dtype) for shape, dtype in shapes]


def from_hbm(*values):
    return [pltpu.with_memory_space_constraint(value, pltpu.HBM) for value in values]


def in_vmem(count):
    return [pl.BlockSpec(memory_space=pltpu.VMEM)] * count


def in_smem(count):
    return [pl.BlockSpec(memory_space=pltpu.SMEM)] * count


def swap(value, peer):
    if peer == 0:
        return value
    pairs = [(source, source ^ peer) for source in range(lax.axis_size("expert"))]
    return lax.ppermute(value, "expert", pairs)


def after(value, first):
    return lax.optimization_barrier((value, first))[0]


def load_weights(params, *weights):
    return pl.pallas_call(
        load_kernel,
        name="load_weights",
        out_shape=results(True, *[(w.shape, w.dtype) for w in weights]),
        in_specs=[pl.BlockSpec(memory_space=pltpu.HBM)] * len(weights),
        out_specs=in_vmem(len(weights)),
        scratch_shapes=[pltpu.SemaphoreType.DMA((len(weights),))],
        cost_estimate=pl.CostEstimate(
            flops=0, bytes_accessed=sum(w.size * 4 for w in weights), transcendentals=0
        ),
        compiler_params=params,
    )(*from_hbm(*weights))


def exchange_all(value):
    return lax.all_to_all(value, "expert", split_axis=0, concat_axis=0, tiled=True)


def shards(
    query,
    keys,
    values,
    lengths,
    routes,
    gates,
    norm_gain,
    old_holds,
    dup_experts,
    w_gate,
    w_up,
    w_down,
):
    width = lax.axis_size("expert")
    batches, tokens, features = query.shape
    lanes = batches * tokens
    cols = features * CAP // PACK
    hidden = w_gate.shape[2]
    relative = width == PERMUTED_WIDTH
    groups = PEER_GROUPS if relative else [list(range(width))]
    order = [peer for group in groups for peer in group]
    block = GROUPS * PACK
    piece = block if relative else block * width
    counts = [len(group) * block // piece for group in groups]
    params = pltpu.CompilerParams(vmem_limit_bytes=24 * MIB if relative else 56 * MIB)
    routes = jnp.transpose(routes, (2, 0, 1))
    gates = jnp.transpose(gates, (2, 0, 1))

    hbm = [pl.BlockSpec(memory_space=pltpu.HBM)] if relative else []
    one = [pltpu.SemaphoreType.DMA(())] if relative else []
    weight = [(w_gate.shape, w_gate.dtype)] if relative else []
    front = pl.pallas_call(
        functools.partial(front_kernel, order, relative),
        name="attend_and_pack",
        out_shape=results(
            relative,
            *weight,
            ((batches, tokens, features), F32),
            *[((piece, cols), BF16)] * sum(counts),
        ),
        in_specs=in_smem(3) + in_vmem(5) + hbm,
        out_specs=in_vmem(len(weight) + 1 + sum(counts)),
        scratch_shapes=[pltpu.VMEM((lanes, features), BF16)] + one,
        compiler_params=params,
    )(
        *from_hbm(lengths, old_holds, dup_experts, query, keys, values, routes, norm_gain),
        *from_hbm(*[w_gate] * len(weight)),
    )
    gate_mat, attn, *send = front if relative else (w_gate, *front)
    sent = dict(zip(order, send))
    arrived = {}
    up_mat, down_mat = w_up, w_down
    if relative:
        half = width // 2
        for peer in groups[0]:
            arrived[peer] = swap(sent[peer], peer)
        up_mat, down_mat = load_weights(params, *[after(w, sent[0]) for w in (w_up, w_down)])
        for peer in groups[1]:
            if peer >= half:
                arrived[peer] = swap(after(sent[peer], down_mat), peer)
        for peer in groups[1]:
            if peer < half:
                arrived[peer] = swap(after(sent[peer], down_mat), peer)
    else:
        arrived[0] = exchange_all(send[0])

    returned = []
    for group, count in zip(groups, counts):
        got = [arrived[peer] for peer in group[:count]]
        rows = min(count * piece, block * 8)
        back = pl.pallas_call(
            functools.partial(expert_kernel, count),
            name="expert_ffn",
            out_shape=results(relative, *[((piece, cols), BF16)] * count),
            in_specs=in_vmem(3 + count),
            out_specs=in_vmem(count),
            scratch_shapes=[pltpu.VMEM((rows, features), BF16), pltpu.VMEM((rows, hidden), BF16)],
            cost_estimate=pl.CostEstimate(
                flops=count * piece * features * hidden * 6,
                bytes_accessed=w_gate.size * 6,
                transcendentals=0,
            ),
            compiler_params=params,
        )(gate_mat, up_mat, down_mat, *got)
        if relative:
            returned.append([swap(part, peer) for part, peer in zip(back, group)])
        else:
            returned.append([exchange_all(part) for part in back])

    mixes = pl.pallas_call(
        functools.partial(weights_kernel, order, relative),
        name="gate_weights",
        out_shape=results(
            relative,
            *[((SPLIT, 2 * lanes, 2 * len(group) * block), BF16) for group in groups],
        ),
        in_specs=in_smem(2) + in_vmem(2),
        out_specs=in_vmem(len(groups)),
        cost_estimate=pl.CostEstimate(flops=0, bytes_accessed=4 * MIB, transcendentals=0),
        compiler_params=params,
    )(*from_hbm(old_holds, dup_experts, after(routes, back[0]), gates))

    base = attn
    for at, (mix, back) in enumerate(zip(mixes, returned)):
        last = at == len(groups) - 1
        base = pl.pallas_call(
            combine_kernel,
            name="combine",
            out_shape=jax.ShapeDtypeStruct(attn.shape, BF16 if last else F32),
            in_specs=in_vmem(2 + len(back)),
            out_specs=in_vmem(1)[0],
            cost_estimate=pl.CostEstimate(
                flops=2 * mix.size * features // SPLIT,
                bytes_accessed=attn.size * 8,
                transcendentals=0,
            ),
            compiler_params=params,
        )(base, mix, *back)
    return base


def solution(mesh):
    placed = (
        P(None, ("dp", "expert"), None),
        P(None, ("dp", "expert"), None),
        P(None, ("dp", "expert"), None),
        P(None, ("dp", "expert"), None),
        P(None, ("dp", "expert"), None),
        P(None, ("dp", "expert"), None),
        P(),
        P(),
        P(),
        P("expert", None, None),
        P("expert", None, None),
        P("expert", None, None),
    )
    return jax.shard_map(
        shards,
        mesh=mesh,
        in_specs=placed,
        out_specs=P(None, ("dp", "expert"), None),
        check_vma=False,
    )
```

```python
import functools
import math

import jax
import jax.numpy as jnp
from jax import lax
from jax.experimental import pallas as pl
from jax.experimental.pallas import tpu as pltpu
from jax.sharding import PartitionSpec as P

HEAD_WIDTH = 128
CAP = 6
PACK = 8
SPLIT = CAP // (PACK - CAP)
GROUPS = 3
PERMUTED_WIDTH = 8
PEER_GROUPS = [[4, 7, 1, 0], [5, 6, 2, 3]]
MIB = 1024 * 1024

F32 = jnp.float32
BF16 = jnp.bfloat16


def dot(a, b, dims=((1,), (0,))):
    return lax.dot_general(a, b, (dims, ((), ())), preferred_element_type=F32)


def row_iota(shape, axis):
    return lax.broadcasted_iota(jnp.int32, shape, axis)


def count_steps(value, step, upto):
    total = jnp.zeros_like(value)
    for at in range(1, upto):
        total = total + (value >= step * at).astype(jnp.int32)
    return total


def slot_picks(order, relative, holds_ref, dup_ref, routes_ref):
    _, batches, tokens = routes_ref.shape
    lanes = batches * tokens
    shape = (len(order), lanes)
    block = row_iota(shape, 0)
    me = lax.axis_index("expert") if relative else 0
    expert = jnp.zeros(shape, jnp.int32)
    for at, slot in enumerate(order):
        expert = jnp.where(block == at, holds_ref[me ^ slot], expert)
    limit = jnp.full(shape, CAP, jnp.int32)
    for at in range(dup_ref.shape[0]):
        limit = jnp.where(expert == dup_ref[at], 2 * CAP, limit)
    limit = jnp.where(row_iota(shape, 1) >= tokens, limit, CAP)
    routes = routes_ref[...]
    routes = jnp.concatenate([routes[:, at, :] for at in range(batches)], axis=1)
    named = [routes[k : k + 1, :] == expert for k in range(routes.shape[0])]
    hit = functools.reduce(jnp.logical_or, named)
    earlier = row_iota((lanes, lanes), 0)
    later = row_iota((lanes, lanes), 1)
    same = (earlier >= tokens) == (later >= tokens)
    before_mat = jnp.where((earlier < later) & same, 1.0, 0.0).astype(BF16)
    before = dot(jnp.where(hit, 1.0, 0.0).astype(BF16), before_mat).astype(jnp.int32)
    before = jnp.where(hit & (before < limit), before, -1)

    shape = (GROUPS * PACK, lanes)
    row = row_iota(shape, 0)
    group = count_steps(row, PACK, GROUPS)
    place = row - group * PACK
    mine = (row_iota(shape, 1) >= tokens) == (group >= 1)
    first = jnp.where(group == 2, CAP, 0)
    lead_place = jnp.where(mine & (place < CAP), place + first, -2)
    trail_places = [
        jnp.where(mine & (place >= CAP), (place - CAP) * SPLIT + piece + first, -2)
        for piece in range(SPLIT)
    ]

    def matches(places):
        blocks = [
            jnp.where(before[at : at + 1, :] == places, 1.0, 0.0) for at in range(len(order))
        ]
        return jnp.concatenate(blocks, axis=0)

    return matches(lead_place), [matches(places) for places in trail_places], named


def attend(query_ref, key_ref, value_ref, lengths_ref, batch, attn_ref):
    tokens = query_ref.shape[1]
    kv_heads = key_ref.shape[2] // HEAD_WIDTH
    group = query_ref.shape[2] // HEAD_WIDTH // kv_heads
    at_row = row_iota((tokens, tokens), 0)
    at_col = row_iota((tokens, tokens), 1)
    row_request = jnp.zeros((tokens, tokens), jnp.int32)
    col_request = jnp.zeros((tokens, tokens), jnp.int32)
    end = jnp.int32(0)
    for r in range(lengths_ref.shape[2]):
        end = end + lengths_ref[batch, 0, r]
        row_request = row_request + (at_row >= end).astype(jnp.int32)
        col_request = col_request + (at_col >= end).astype(jnp.int32)
    allowed = (row_request == col_request) & (at_col <= at_row)
    bias = jnp.where(allowed, 0.0, -1e30)
    scale = HEAD_WIDTH ** (-0.5) * math.log2(math.e)
    squares = jnp.zeros((tokens, HEAD_WIDTH), F32)
    for h in range(kv_heads):
        kv = slice(h * HEAD_WIDTH, (h + 1) * HEAD_WIDTH)
        heads = [
            slice((h * group + g) * HEAD_WIDTH, (h * group + g + 1) * HEAD_WIDTH)
            for g in range(group)
        ]
        q = jnp.concatenate([query_ref[batch, :, cols] for cols in heads], axis=0)
        scores = dot(q, key_ref[batch, :, kv], ((1,), (1,)))
        scores = scores.reshape(group, tokens, tokens) + bias[None]
        weights = jnp.exp2((scores - jnp.max(scores, axis=-1, keepdims=True)) * scale)
        share = 1.0 / jnp.sum(weights, axis=-1, keepdims=True)
        probs = (weights * share).astype(BF16)
        mixed = dot(probs.reshape(group * tokens, tokens), value_ref[batch, :, kv])
        for g, cols in enumerate(heads):
            part = mixed[g * tokens : (g + 1) * tokens]
            attn_ref[batch, :, cols] = part
            squares = squares + part * part
    meansq = jnp.sum(squares, axis=-1, keepdims=True) / query_ref.shape[2]
    return lax.rsqrt(meansq + 1e-05)


def front_kernel(order, relative, *refs):
    sources, refs = refs[:8], refs[8:]
    if relative:
        gate_hbm, gate_ref, attn_ref, *refs = refs
    else:
        attn_ref, *refs = refs
    send_refs, refs = refs[: -(len(sources) + 2)], refs[-(len(sources) + 2) :]
    *targets, normed_ref, sems = refs
    lengths_ref, holds_ref, dup_ref, routes_ref, gain_ref, query_ref, key_ref, value_ref = targets
    batches, tokens, features = query_ref.shape
    piece, cols = send_refs[0].shape
    step = cols // SPLIT

    small = [pltpu.make_async_copy(sources[i], targets[i], sems.at[0, i]) for i in range(5)]
    large = [
        [
            pltpu.make_async_copy(sources[i].at[b], targets[i].at[b], sems.at[1 + b, i])
            for i in range(5, 8)
        ]
        for b in range(batches)
    ]
    for copy in small + [copy for copies in large for copy in copies]:
        copy.start()
    if relative:
        load = pltpu.make_async_copy(gate_hbm, gate_ref, sems.at[1, 0])
        load.start()
    for copy in small:
        copy.wait()

    @pl.when(holds_ref[0] >= 0)
    def _():
        lead, trail, _ = slot_picks(order, relative, holds_ref, dup_ref, routes_ref)
        for b in range(batches):
            for copy in large[b]:
                copy.wait()
        for b in range(batches):
            scale = attend(query_ref, key_ref, value_ref, lengths_ref, b, attn_ref)
            normed_ref[b * tokens : (b + 1) * tokens, :] = (
                attn_ref[b] * scale * gain_ref[...][None, :]
            ).astype(BF16)
        tail = normed_ref[:, cols:features]
        for j in range(SPLIT):
            at = slice(j * step, (j + 1) * step)
            picks = jnp.concatenate([lead, trail[j]], axis=1).astype(BF16)
            source = jnp.concatenate([normed_ref[:, at], tail], axis=0)
            packed = dot(picks, source)
            for i, send_ref in enumerate(send_refs):
                send_ref[:, at] = packed[i * piece : (i + 1) * piece].astype(BF16)

    if relative:
        load.wait()


def load_kernel(*refs):
    *refs, sems = refs
    half = len(refs) // 2
    loads = [
        pltpu.make_async_copy(refs[i], refs[half + i], sems.at[i]) for i in range(half)
    ]
    for load in loads:
        load.start()
    for load in loads:
        load.wait()


def weights_kernel(order, relative, holds_ref, dup_ref, routes_ref, gates_ref, *mix_refs):
    lead, trail, named = slot_picks(order, relative, holds_ref, dup_ref, routes_ref)
    gates = gates_ref[...]
    gates = jnp.concatenate([gates[:, at, :] for at in range(gates.shape[1])], axis=1)
    gate = jnp.zeros(named[0].shape, F32)
    for k, match in enumerate(named):
        gate = gate + jnp.where(match, gates[k : k + 1, :], 0.0)
    high = gate.astype(BF16).astype(F32)
    lanes = lead.shape[1]
    rows = mix_refs[0].shape[2] // 2
    block = GROUPS * PACK
    for k, part in enumerate((high, gate - high)):
        spread = [jnp.broadcast_to(part[at : at + 1], (block, lanes)) for at in range(len(order))]
        spread = jnp.concatenate(spread, axis=0)
        for j in range(SPLIT):
            for half, pick in enumerate((lead, trail[j])):
                weight = pick * spread
                for i, mix_ref in enumerate(mix_refs):
                    mix_ref[j, half * lanes : (half + 1) * lanes, k * rows : (k + 1) * rows] = (
                        weight[i * rows : (i + 1) * rows].T.astype(BF16)
                    )


def expert_kernel(count, gate_ref, up_ref, down_ref, *rest):
    got_refs, back_refs = rest[:count], rest[count : 2 * count]
    rows_ref, hidden_ref = rest[2 * count :]
    piece, cols = got_refs[0].shape
    features = rows_ref.shape[1]
    step = cols // SPLIT
    block, hidden = hidden_ref.shape
    shape = (block, block)
    row = row_iota(shape, 0)
    other = row_iota(shape, 1)
    place = lax.rem(row, PACK)
    tile = row - place

    def trails(j):
        picked = jnp.zeros(shape, jnp.bool_)
        for a in range(PACK - CAP):
            picked = picked | ((place == a * SPLIT + j) & (other == tile + CAP + a))
        return jnp.where(picked, 1.0, 0.0).astype(BF16)

    take = min(piece, block)
    for start in range(0, piece * count, block):
        spots = [
            (at // piece, slice(at % piece, at % piece + take), slice(at - start, at - start + take))
            for at in range(start, start + block, take)
        ]
        for i, theirs, mine in spots:
            rows_ref[mine, :cols] = got_refs[i][theirs, :]
        tail = jnp.zeros((block, features - cols), F32)
        for j in range(SPLIT):
            tail = tail + dot(trails(j), rows_ref[:, j * step : (j + 1) * step])
        rows_ref[:, cols:] = tail.astype(BF16)
        chunk = 256 if hidden % 256 == 0 else hidden
        for c in range(0, hidden, chunk):
            gate_val = dot(rows_ref[...], gate_ref[0, :, c : c + chunk])
            up_val = dot(rows_ref[...], up_ref[0, :, c : c + chunk])
            hidden_ref[:, c : c + chunk] = (
                gate_val / (1.0 + jnp.exp(-gate_val)) * up_val
            ).astype(BF16)
        tail = dot(hidden_ref[...], down_ref[0, :, cols:]).astype(BF16)
        leading = lax.rem(row_iota((block, step), 0), PACK) < CAP
        for j in range(SPLIT):
            at = slice(j * step, (j + 1) * step)
            moved = dot(trails(j), tail, ((0,), (0,)))
            result = jnp.where(leading, dot(hidden_ref[...], down_ref[0, :, at]), moved)
            for i, theirs, mine in spots:
                back_refs[i][theirs, at] = result[mine].astype(BF16)


def combine_kernel(last, base_ref, mix_ref, *rest):
    if last:
        *back_refs, out_hbm, out_ref, sems = rest
    else:
        *back_refs, out_ref = rest
    batches, tokens, features = base_ref.shape
    lanes = batches * tokens
    piece, cols = back_refs[0].shape
    step = cols // SPLIT
    tail = jnp.zeros((lanes, features - cols), F32)

    def write(index, at):
        return pltpu.make_async_copy(out_ref.at[:, :, at], out_hbm.at[:, :, at], sems.at[index])

    def put(part, index, at):
        for b in range(batches):
            out_ref[b, :, at] = (base_ref[b, :, at] + part[b * tokens : (b + 1) * tokens]).astype(
                out_ref.dtype
            )
        if last:
            write(index, at).start()

    def columns(j):
        return pl.ds(j * step, step)

    for j in range(SPLIT):
        at = columns(j)
        back = jnp.concatenate([back_ref[:, at] for back_ref in back_refs] * 2, axis=0)
        mixed = dot(mix_ref[j], back)
        put(mixed[:lanes], j, at)
        tail = tail + mixed[lanes:]
    rest_at = pl.ds(cols, features - cols)
    put(tail, SPLIT, rest_at)
    if last:
        for j in range(SPLIT):
            write(j, columns(j)).wait()
        write(SPLIT, rest_at).wait()


def results(in_vmem, *shapes):
    kind = pltpu.VMEM if in_vmem else jax.ShapeDtypeStruct
    return [kind(shape, dtype) for shape, dtype in shapes]


def from_hbm(*values):
    return [pltpu.with_memory_space_constraint(value, pltpu.HBM) for value in values]


def in_vmem(count):
    return [pl.BlockSpec(memory_space=pltpu.VMEM)] * count


def in_smem(count):
    return [pl.BlockSpec(memory_space=pltpu.SMEM)] * count


def swap(value, peer):
    if peer == 0:
        return value
    pairs = [(source, source ^ peer) for source in range(lax.axis_size("expert"))]
    return lax.ppermute(value, "expert", pairs)


def after(value, first):
    return lax.optimization_barrier((value, first))[0]


def load_weights(params, *weights):
    return pl.pallas_call(
        load_kernel,
        name="load_weights",
        out_shape=results(True, *[(w.shape, w.dtype) for w in weights]),
        in_specs=[pl.BlockSpec(memory_space=pltpu.HBM)] * len(weights),
        out_specs=in_vmem(len(weights)),
        scratch_shapes=[pltpu.SemaphoreType.DMA((len(weights),))],
        cost_estimate=pl.CostEstimate(
            flops=0, bytes_accessed=sum(w.size * 4 for w in weights), transcendentals=0
        ),
        compiler_params=params,
    )(*from_hbm(*weights))


def exchange_all(value):
    return lax.all_to_all(value, "expert", split_axis=0, concat_axis=0, tiled=True)


def shards(
    query,
    keys,
    values,
    lengths,
    routes,
    gates,
    norm_gain,
    old_holds,
    dup_experts,
    w_gate,
    w_up,
    w_down,
):
    width = lax.axis_size("expert")
    batches, tokens, features = query.shape
    lanes = batches * tokens
    cols = features * CAP // PACK
    hidden = w_gate.shape[2]
    relative = width == PERMUTED_WIDTH
    groups = PEER_GROUPS if relative else [list(range(width))]
    order = [peer for group in groups for peer in group]
    block = GROUPS * PACK
    piece = block if relative else block * width
    counts = [len(group) * block // piece for group in groups]
    params = pltpu.CompilerParams(vmem_limit_bytes=24 * MIB if relative else 56 * MIB)
    routes = jnp.transpose(routes, (2, 0, 1))
    gates = jnp.transpose(gates, (2, 0, 1))

    weight = [(w_gate.shape, w_gate.dtype)] if relative else []
    front_args = from_hbm(
        lengths, old_holds, dup_experts, routes, norm_gain, query, keys, values,
        *[w_gate] * len(weight),
    )
    front = pl.pallas_call(
        functools.partial(front_kernel, order, relative),
        name="attend_and_pack",
        out_shape=results(
            relative,
            *weight,
            ((batches, tokens, features), F32),
            *[((piece, cols), BF16)] * sum(counts),
        ),
        in_specs=[pl.BlockSpec(memory_space=pltpu.HBM)] * len(front_args),
        out_specs=in_vmem(len(weight) + 1 + sum(counts)),
        scratch_shapes=[pltpu.SMEM(x.shape, x.dtype) for x in front_args[:3]]
        + [pltpu.VMEM(x.shape, x.dtype) for x in front_args[3:8]]
        + [pltpu.VMEM((lanes, features), BF16), pltpu.SemaphoreType.DMA((1 + batches, 8))],
        compiler_params=params,
    )(*front_args)
    gate_mat, attn, *send = front if relative else (w_gate, *front)
    sent = dict(zip(order, send))
    arrived = {}
    up_mat, down_mat = w_up, w_down
    if relative:
        half = width // 2
        for peer in groups[0]:
            arrived[peer] = swap(sent[peer], peer)
        up_mat, down_mat = load_weights(params, *[after(w, sent[0]) for w in (w_up, w_down)])
        for peer in groups[1]:
            if peer >= half:
                arrived[peer] = swap(after(sent[peer], down_mat), peer)
        for peer in groups[1]:
            if peer < half:
                arrived[peer] = swap(after(sent[peer], down_mat), peer)
    else:
        arrived[0] = exchange_all(send[0])

    returned = []
    for group, count in zip(groups, counts):
        got = [arrived[peer] for peer in group[:count]]
        rows = min(count * piece, block * 8)
        back = pl.pallas_call(
            functools.partial(expert_kernel, count),
            name="expert_ffn",
            out_shape=results(relative, *[((piece, cols), BF16)] * count),
            in_specs=in_vmem(3 + count),
            out_specs=in_vmem(count),
            scratch_shapes=[pltpu.VMEM((rows, features), BF16), pltpu.VMEM((rows, hidden), BF16)],
            cost_estimate=pl.CostEstimate(
                flops=count * piece * features * hidden * 6,
                bytes_accessed=w_gate.size * 6,
                transcendentals=0,
            ),
            compiler_params=params,
        )(gate_mat, up_mat, down_mat, *got)
        if relative:
            returned.append([swap(part, peer) for part, peer in zip(back, group)])
        else:
            returned.append([exchange_all(part) for part in back])

    mixes = pl.pallas_call(
        functools.partial(weights_kernel, order, relative),
        name="gate_weights",
        out_shape=results(
            relative,
            *[((SPLIT, 2 * lanes, 2 * len(group) * block), BF16) for group in groups],
        ),
        in_specs=in_smem(2) + in_vmem(2),
        out_specs=in_vmem(len(groups)),
        cost_estimate=pl.CostEstimate(flops=0, bytes_accessed=4 * MIB, transcendentals=0),
        compiler_params=params,
    )(*from_hbm(old_holds, dup_experts, after(routes, back[0]), gates))

    base = attn
    for at, (mix, back) in enumerate(zip(mixes, returned)):
        last = at == len(groups) - 1
        out = (attn.shape, BF16 if last else F32)
        base = pl.pallas_call(
            functools.partial(combine_kernel, last),
            name="combine",
            out_shape=results(relative and not last, out)[0],
            in_specs=in_vmem(2 + len(back)),
            out_specs=pl.BlockSpec(memory_space=pltpu.HBM) if last else in_vmem(1)[0],
            scratch_shapes=[pltpu.VMEM(*out)] * last
            + [pltpu.SemaphoreType.DMA((SPLIT + 1,))] * last,
            cost_estimate=pl.CostEstimate(
                flops=2 * mix.size * features // SPLIT,
                bytes_accessed=attn.size * 8,
                transcendentals=0,
            ),
            compiler_params=params,
        )(base, mix, *back)
    return base


def solution(mesh):
    placed = (
        P(None, ("dp", "expert"), None),
        P(None, ("dp", "expert"), None),
        P(None, ("dp", "expert"), None),
        P(None, ("dp", "expert"), None),
        P(None, ("dp", "expert"), None),
        P(None, ("dp", "expert"), None),
        P(),
        P(),
        P(),
        P("expert", None, None),
        P("expert", None, None),
        P("expert", None, None),
    )
    return jax.shard_map(
        shards,
        mesh=mesh,
        in_specs=placed,
        out_specs=P(None, ("dp", "expert"), None),
        check_vma=False,
    )
```

```python
import functools
import math

import jax
import jax.numpy as jnp
from jax import lax
from jax.experimental import pallas as pl
from jax.experimental.pallas import tpu as pltpu
from jax.sharding import PartitionSpec as P

HEAD_WIDTH = 128
CAP = 6
PACK = 8
SPLIT = CAP // (PACK - CAP)
GROUPS = 3
PERMUTED_WIDTH = 8
PEER_GROUPS = [[4, 7, 1, 0], [5, 6, 2, 3]]
MIB = 1024 * 1024

F32 = jnp.float32
BF16 = jnp.bfloat16


def dot(a, b, dims=((1,), (0,))):
    return lax.dot_general(a, b, (dims, ((), ())), preferred_element_type=F32)


def row_iota(shape, axis):
    return lax.broadcasted_iota(jnp.int32, shape, axis)


def count_steps(value, step, upto):
    total = jnp.zeros_like(value)
    for at in range(1, upto):
        total = total + (value >= step * at).astype(jnp.int32)
    return total


def slot_picks(order, relative, holds_ref, dup_ref, routes_ref):
    _, batches, tokens = routes_ref.shape
    lanes = batches * tokens
    shape = (len(order), lanes)
    block = row_iota(shape, 0)
    me = lax.axis_index("expert") if relative else 0
    expert = jnp.zeros(shape, jnp.int32)
    for at, slot in enumerate(order):
        expert = jnp.where(block == at, holds_ref[me ^ slot], expert)
    limit = jnp.full(shape, CAP, jnp.int32)
    for at in range(dup_ref.shape[0]):
        limit = jnp.where(expert == dup_ref[at], 2 * CAP, limit)
    limit = jnp.where(row_iota(shape, 1) >= tokens, limit, CAP)
    routes = routes_ref[...]
    routes = jnp.concatenate([routes[:, at, :] for at in range(batches)], axis=1)
    named = [routes[k : k + 1, :] == expert for k in range(routes.shape[0])]
    hit = functools.reduce(jnp.logical_or, named)
    earlier = row_iota((lanes, lanes), 0)
    later = row_iota((lanes, lanes), 1)
    same = (earlier >= tokens) == (later >= tokens)
    before_mat = jnp.where((earlier < later) & same, 1.0, 0.0).astype(BF16)
    before = dot(jnp.where(hit, 1.0, 0.0).astype(BF16), before_mat).astype(jnp.int32)
    before = jnp.where(hit & (before < limit), before, -1)

    shape = (GROUPS * PACK, lanes)
    row = row_iota(shape, 0)
    group = count_steps(row, PACK, GROUPS)
    place = row - group * PACK
    mine = (row_iota(shape, 1) >= tokens) == (group >= 1)
    first = jnp.where(group == 2, CAP, 0)
    lead_place = jnp.where(mine & (place < CAP), place + first, -2)
    trail_places = [
        jnp.where(mine & (place >= CAP), (place - CAP) * SPLIT + piece + first, -2)
        for piece in range(SPLIT)
    ]

    def matches(places):
        blocks = [
            jnp.where(before[at : at + 1, :] == places, 1.0, 0.0) for at in range(len(order))
        ]
        return jnp.concatenate(blocks, axis=0)

    return matches(lead_place), [matches(places) for places in trail_places], named


def attend(query_ref, key_ref, value_ref, lengths_ref, batch, attn_ref):
    tokens = query_ref.shape[1]
    kv_heads = key_ref.shape[2] // HEAD_WIDTH
    group = query_ref.shape[2] // HEAD_WIDTH // kv_heads
    at_row = row_iota((tokens, tokens), 0)
    at_col = row_iota((tokens, tokens), 1)
    row_request = jnp.zeros((tokens, tokens), jnp.int32)
    col_request = jnp.zeros((tokens, tokens), jnp.int32)
    end = jnp.int32(0)
    for r in range(lengths_ref.shape[2]):
        end = end + lengths_ref[batch, 0, r]
        row_request = row_request + (at_row >= end).astype(jnp.int32)
        col_request = col_request + (at_col >= end).astype(jnp.int32)
    allowed = (row_request == col_request) & (at_col <= at_row)
    bias = jnp.where(allowed, 0.0, -1e30)
    scale = HEAD_WIDTH ** (-0.5) * math.log2(math.e)
    squares = jnp.zeros((tokens, HEAD_WIDTH), F32)
    for h in range(kv_heads):
        kv = slice(h * HEAD_WIDTH, (h + 1) * HEAD_WIDTH)
        heads = [
            slice((h * group + g) * HEAD_WIDTH, (h * group + g + 1) * HEAD_WIDTH)
            for g in range(group)
        ]
        q = jnp.concatenate([query_ref[batch, :, cols] for cols in heads], axis=0)
        scores = dot(q, key_ref[batch, :, kv], ((1,), (1,)))
        scores = scores.reshape(group, tokens, tokens) + bias[None]
        weights = jnp.exp2((scores - jnp.max(scores, axis=-1, keepdims=True)) * scale)
        share = 1.0 / jnp.sum(weights, axis=-1, keepdims=True)
        probs = (weights * share).astype(BF16)
        mixed = dot(probs.reshape(group * tokens, tokens), value_ref[batch, :, kv])
        for g, cols in enumerate(heads):
            part = mixed[g * tokens : (g + 1) * tokens]
            attn_ref[batch, :, cols] = part
            squares = squares + part * part
    meansq = jnp.sum(squares, axis=-1, keepdims=True) / query_ref.shape[2]
    return lax.rsqrt(meansq + 1e-05)


def front_kernel(order, relative, *refs):
    sources, refs = refs[:8], refs[8:]
    if relative:
        gate_hbm, gate_ref, attn_ref, *refs = refs
    else:
        attn_ref, *refs = refs
    send_refs, refs = refs[: -(len(sources) + 2)], refs[-(len(sources) + 2) :]
    *targets, normed_ref, sems = refs
    lengths_ref, holds_ref, dup_ref, routes_ref, gain_ref, query_ref, key_ref, value_ref = targets
    batches, tokens, features = query_ref.shape
    piece, cols = send_refs[0].shape
    step = cols // SPLIT

    small = [pltpu.make_async_copy(sources[i], targets[i], sems.at[0, i]) for i in range(5)]
    large = [
        [
            pltpu.make_async_copy(sources[i].at[b], targets[i].at[b], sems.at[1 + b, i])
            for i in range(5, 8)
        ]
        for b in range(batches)
    ]
    for copy in small + [copy for copies in large for copy in copies]:
        copy.start()
    if relative:
        load = pltpu.make_async_copy(gate_hbm, gate_ref, sems.at[1, 0])
        load.start()
    for copy in small:
        copy.wait()

    @pl.when(holds_ref[0] >= 0)
    def _():
        lead, trail, _ = slot_picks(order, relative, holds_ref, dup_ref, routes_ref)
        for b in range(batches):
            for copy in large[b]:
                copy.wait()
        for b in range(batches):
            scale = attend(query_ref, key_ref, value_ref, lengths_ref, b, attn_ref)
            normed_ref[b * tokens : (b + 1) * tokens, :] = (
                attn_ref[b] * scale * gain_ref[...][None, :]
            ).astype(BF16)
        tail = normed_ref[:, cols:features]
        for j in range(SPLIT):
            at = slice(j * step, (j + 1) * step)
            picks = jnp.concatenate([lead, trail[j]], axis=1).astype(BF16)
            source = jnp.concatenate([normed_ref[:, at], tail], axis=0)
            packed = dot(picks, source)
            for i, send_ref in enumerate(send_refs):
                send_ref[:, at] = packed[i * piece : (i + 1) * piece].astype(BF16)

    if relative:
        load.wait()


def load_kernel(*refs):
    *refs, sems = refs
    half = len(refs) // 2
    loads = [
        pltpu.make_async_copy(refs[i], refs[half + i], sems.at[i]) for i in range(half)
    ]
    for load in loads:
        load.start()
    for load in loads:
        load.wait()


def weights_kernel(order, relative, holds_ref, dup_ref, routes_ref, gates_ref, *mix_refs):
    lead, trail, named = slot_picks(order, relative, holds_ref, dup_ref, routes_ref)
    gates = gates_ref[...]
    gates = jnp.concatenate([gates[:, at, :] for at in range(gates.shape[1])], axis=1)
    gate = jnp.zeros(named[0].shape, F32)
    for k, match in enumerate(named):
        gate = gate + jnp.where(match, gates[k : k + 1, :], 0.0)
    high = gate.astype(BF16).astype(F32)
    lanes = lead.shape[1]
    rows = mix_refs[0].shape[2] // 2
    block = GROUPS * PACK
    for k, part in enumerate((high, gate - high)):
        spread = [jnp.broadcast_to(part[at : at + 1], (block, lanes)) for at in range(len(order))]
        spread = jnp.concatenate(spread, axis=0)
        for j in range(SPLIT):
            for half, pick in enumerate((lead, trail[j])):
                weight = pick * spread
                for i, mix_ref in enumerate(mix_refs):
                    mix_ref[j, half * lanes : (half + 1) * lanes, k * rows : (k + 1) * rows] = (
                        weight[i * rows : (i + 1) * rows].T.astype(BF16)
                    )


def expert_kernel(count, gate_ref, up_ref, down_ref, *rest):
    got_refs, back_refs = rest[:count], rest[count : 2 * count]
    rows_ref, hidden_ref = rest[2 * count :]
    piece, cols = got_refs[0].shape
    features = rows_ref.shape[1]
    step = cols // SPLIT
    block, hidden = hidden_ref.shape
    shape = (block, block)
    row = row_iota(shape, 0)
    other = row_iota(shape, 1)
    place = lax.rem(row, PACK)
    tile = row - place

    def trails(j):
        picked = jnp.zeros(shape, jnp.bool_)
        for a in range(PACK - CAP):
            picked = picked | ((place == a * SPLIT + j) & (other == tile + CAP + a))
        return jnp.where(picked, 1.0, 0.0).astype(BF16)

    take = min(piece, block)
    for start in range(0, piece * count, block):
        spots = [
            (at // piece, slice(at % piece, at % piece + take), slice(at - start, at - start + take))
            for at in range(start, start + block, take)
        ]
        for i, theirs, mine in spots:
            rows_ref[mine, :cols] = got_refs[i][theirs, :]
        tail = jnp.zeros((block, features - cols), F32)
        for j in range(SPLIT):
            tail = tail + dot(trails(j), rows_ref[:, j * step : (j + 1) * step])
        rows_ref[:, cols:] = tail.astype(BF16)
        chunk = 256 if hidden % 256 == 0 else hidden
        for c in range(0, hidden, chunk):
            gate_val = dot(rows_ref[...], gate_ref[0, :, c : c + chunk])
            up_val = dot(rows_ref[...], up_ref[0, :, c : c + chunk])
            hidden_ref[:, c : c + chunk] = (
                gate_val / (1.0 + jnp.exp(-gate_val)) * up_val
            ).astype(BF16)
        tail = dot(hidden_ref[...], down_ref[0, :, cols:]).astype(BF16)
        leading = lax.rem(row_iota((block, step), 0), PACK) < CAP
        for j in range(SPLIT):
            at = slice(j * step, (j + 1) * step)
            moved = dot(trails(j), tail, ((0,), (0,)))
            result = jnp.where(leading, dot(hidden_ref[...], down_ref[0, :, at]), moved)
            for i, theirs, mine in spots:
                back_refs[i][theirs, at] = result[mine].astype(BF16)


def combine_kernel(last, base_ref, mix_ref, *rest):
    if last:
        *back_refs, out_hbm, out_ref, sems = rest
    else:
        *back_refs, out_ref = rest
    batches, tokens, features = base_ref.shape
    lanes = batches * tokens
    piece, cols = back_refs[0].shape
    step = cols // SPLIT
    tail = jnp.zeros((lanes, features - cols), F32)

    def write(index, at):
        return pltpu.make_async_copy(out_ref.at[:, :, at], out_hbm.at[:, :, at], sems.at[index])

    def put(part, index, at):
        for b in range(batches):
            out_ref[b, :, at] = (base_ref[b, :, at] + part[b * tokens : (b + 1) * tokens]).astype(
                out_ref.dtype
            )
        if last:
            write(index, at).start()

    def columns(j):
        return pl.ds(j * step, step)

    for j in range(SPLIT):
        at = columns(j)
        back = jnp.concatenate([back_ref[:, at] for back_ref in back_refs] * 2, axis=0)
        mixed = dot(mix_ref[j], back)
        put(mixed[:lanes], j, at)
        tail = tail + mixed[lanes:]
    rest_at = pl.ds(cols, features - cols)
    put(tail, SPLIT, rest_at)
    if last:
        for j in range(SPLIT):
            write(j, columns(j)).wait()
        write(SPLIT, rest_at).wait()


def results(in_vmem, *shapes):
    kind = pltpu.VMEM if in_vmem else jax.ShapeDtypeStruct
    return [kind(shape, dtype) for shape, dtype in shapes]


def from_hbm(*values):
    return [pltpu.with_memory_space_constraint(value, pltpu.HBM) for value in values]


def in_vmem(count):
    return [pl.BlockSpec(memory_space=pltpu.VMEM)] * count


def in_smem(count):
    return [pl.BlockSpec(memory_space=pltpu.SMEM)] * count


def swap(value, peer):
    if peer == 0:
        return value
    pairs = [(source, source ^ peer) for source in range(lax.axis_size("expert"))]
    return lax.ppermute(value, "expert", pairs)


def after(value, first):
    return lax.optimization_barrier((value, first))[0]


def load_weights(params, *weights):
    return pl.pallas_call(
        load_kernel,
        name="load_weights",
        out_shape=results(True, *[(w.shape, w.dtype) for w in weights]),
        in_specs=[pl.BlockSpec(memory_space=pltpu.HBM)] * len(weights),
        out_specs=in_vmem(len(weights)),
        scratch_shapes=[pltpu.SemaphoreType.DMA((len(weights),))],
        cost_estimate=pl.CostEstimate(
            flops=0, bytes_accessed=sum(w.size * 4 for w in weights), transcendentals=0
        ),
        compiler_params=params,
    )(*from_hbm(*weights))


def exchange_all(value):
    return lax.all_to_all(value, "expert", split_axis=0, concat_axis=0, tiled=True)


def shards(
    query,
    keys,
    values,
    lengths,
    routes,
    gates,
    norm_gain,
    old_holds,
    dup_experts,
    w_gate,
    w_up,
    w_down,
):
    width = lax.axis_size("expert")
    batches, tokens, features = query.shape
    lanes = batches * tokens
    cols = features * CAP // PACK
    hidden = w_gate.shape[2]
    relative = width == PERMUTED_WIDTH
    groups = PEER_GROUPS if relative else [list(range(width))]
    order = [peer for group in groups for peer in group]
    block = GROUPS * PACK
    piece = block if relative else block * width
    counts = [len(group) * block // piece for group in groups]
    params = pltpu.CompilerParams(vmem_limit_bytes=24 * MIB if relative else 56 * MIB)
    routes = jnp.transpose(routes, (2, 0, 1))
    gates = jnp.transpose(gates, (2, 0, 1))

    weight = [(w_gate.shape, w_gate.dtype)] if relative else []
    front_args = from_hbm(
        lengths, old_holds, dup_experts, routes, norm_gain, query, keys, values,
        *[w_gate] * len(weight),
    )
    front = pl.pallas_call(
        functools.partial(front_kernel, order, relative),
        name="attend_and_pack",
        out_shape=results(
            relative,
            *weight,
            ((batches, tokens, features), F32),
            *[((piece, cols), BF16)] * sum(counts),
        ),
        in_specs=[pl.BlockSpec(memory_space=pltpu.HBM)] * len(front_args),
        out_specs=in_vmem(len(weight) + 1 + sum(counts)),
        scratch_shapes=[pltpu.SMEM(x.shape, x.dtype) for x in front_args[:3]]
        + [pltpu.VMEM(x.shape, x.dtype) for x in front_args[3:8]]
        + [pltpu.VMEM((lanes, features), BF16), pltpu.SemaphoreType.DMA((1 + batches, 8))],
        compiler_params=params,
    )(*front_args)
    gate_mat, attn, *send = front if relative else (w_gate, *front)
    sent = dict(zip(order, send))
    arrived = {}
    up_mat, down_mat = w_up, w_down
    if relative:
        half = width // 2
        for peer in groups[0]:
            arrived[peer] = swap(sent[peer], peer)
        up_mat, down_mat = load_weights(params, *[after(w, sent[0]) for w in (w_up, w_down)])
        wait = down_mat
        for peer in groups[1]:
            if peer >= half:
                arrived[peer] = swap(after(sent[peer], wait), peer)
                wait = (down_mat, arrived[groups[0][0]])
        for peer in groups[1]:
            if peer < half:
                arrived[peer] = swap(after(sent[peer], down_mat), peer)
    else:
        arrived[0] = exchange_all(send[0])

    returned = []
    for group, count in zip(groups, counts):
        got = [arrived[peer] for peer in group[:count]]
        rows = min(count * piece, block * 8)
        back = pl.pallas_call(
            functools.partial(expert_kernel, count),
            name="expert_ffn",
            out_shape=results(relative, *[((piece, cols), BF16)] * count),
            in_specs=in_vmem(3 + count),
            out_specs=in_vmem(count),
            scratch_shapes=[pltpu.VMEM((rows, features), BF16), pltpu.VMEM((rows, hidden), BF16)],
            cost_estimate=pl.CostEstimate(
                flops=count * piece * features * hidden * 6,
                bytes_accessed=w_gate.size * 6,
                transcendentals=0,
            ),
            compiler_params=params,
        )(gate_mat, up_mat, down_mat, *got)
        if relative:
            returned.append([swap(part, peer) for part, peer in zip(back, group)])
        else:
            returned.append([exchange_all(part) for part in back])

    mixes = pl.pallas_call(
        functools.partial(weights_kernel, order, relative),
        name="gate_weights",
        out_shape=results(
            relative,
            *[((SPLIT, 2 * lanes, 2 * len(group) * block), BF16) for group in groups],
        ),
        in_specs=in_smem(2) + in_vmem(2),
        out_specs=in_vmem(len(groups)),
        cost_estimate=pl.CostEstimate(flops=0, bytes_accessed=4 * MIB, transcendentals=0),
        compiler_params=params,
    )(*from_hbm(old_holds, dup_experts, after(routes, back[0]), gates))

    base = attn
    for at, (mix, back) in enumerate(zip(mixes, returned)):
        last = at == len(groups) - 1
        out = (attn.shape, BF16 if last else F32)
        base = pl.pallas_call(
            functools.partial(combine_kernel, last),
            name="combine",
            out_shape=results(relative and not last, out)[0],
            in_specs=in_vmem(2 + len(back)),
            out_specs=pl.BlockSpec(memory_space=pltpu.HBM) if last else in_vmem(1)[0],
            scratch_shapes=[pltpu.VMEM(*out)] * last
            + [pltpu.SemaphoreType.DMA((SPLIT + 1,))] * last,
            cost_estimate=pl.CostEstimate(
                flops=2 * mix.size * features // SPLIT,
                bytes_accessed=attn.size * 8,
                transcendentals=0,
            ),
            compiler_params=params,
        )(base, mix, *back)
    return base


def solution(mesh):
    placed = (
        P(None, ("dp", "expert"), None),
        P(None, ("dp", "expert"), None),
        P(None, ("dp", "expert"), None),
        P(None, ("dp", "expert"), None),
        P(None, ("dp", "expert"), None),
        P(None, ("dp", "expert"), None),
        P(),
        P(),
        P(),
        P("expert", None, None),
        P("expert", None, None),
        P("expert", None, None),
    )
    return jax.shard_map(
        shards,
        mesh=mesh,
        in_specs=placed,
        out_specs=P(None, ("dp", "expert"), None),
        check_vma=False,
    )
```

```python
import functools
import math

import jax
import jax.numpy as jnp
from jax import lax
from jax.experimental import pallas as pl
from jax.experimental.pallas import tpu as pltpu
from jax.sharding import PartitionSpec as P

HEAD_WIDTH = 128
CAP = 6
PACK = 8
SPLIT = CAP // (PACK - CAP)
GROUPS = 3
PERMUTED_WIDTH = 8
PEER_GROUPS = [[4, 7, 1, 0], [5, 6, 2, 3]]
MIB = 1024 * 1024

F32 = jnp.float32
BF16 = jnp.bfloat16


def dot(a, b, dims=((1,), (0,))):
    return lax.dot_general(a, b, (dims, ((), ())), preferred_element_type=F32)


def row_iota(shape, axis):
    return lax.broadcasted_iota(jnp.int32, shape, axis)


def count_steps(value, step, upto):
    total = jnp.zeros_like(value)
    for at in range(1, upto):
        total = total + (value >= step * at).astype(jnp.int32)
    return total


def slot_picks(order, relative, holds_ref, dup_ref, routes_ref):
    _, batches, tokens = routes_ref.shape
    lanes = batches * tokens
    shape = (len(order), lanes)
    block = row_iota(shape, 0)
    me = lax.axis_index("expert") if relative else 0
    expert = jnp.zeros(shape, jnp.int32)
    for at, slot in enumerate(order):
        expert = jnp.where(block == at, holds_ref[me ^ slot], expert)
    limit = jnp.full(shape, CAP, jnp.int32)
    for at in range(dup_ref.shape[0]):
        limit = jnp.where(expert == dup_ref[at], 2 * CAP, limit)
    limit = jnp.where(row_iota(shape, 1) >= tokens, limit, CAP)
    routes = routes_ref[...]
    routes = jnp.concatenate([routes[:, at, :] for at in range(batches)], axis=1)
    named = [routes[k : k + 1, :] == expert for k in range(routes.shape[0])]
    hit = functools.reduce(jnp.logical_or, named)
    earlier = row_iota((lanes, lanes), 0)
    later = row_iota((lanes, lanes), 1)
    same = (earlier >= tokens) == (later >= tokens)
    before_mat = jnp.where((earlier < later) & same, 1.0, 0.0).astype(BF16)
    before = dot(jnp.where(hit, 1.0, 0.0).astype(BF16), before_mat).astype(jnp.int32)
    before = jnp.where(hit & (before < limit), before, -1)

    shape = (GROUPS * PACK, lanes)
    row = row_iota(shape, 0)
    group = count_steps(row, PACK, GROUPS)
    place = row - group * PACK
    mine = (row_iota(shape, 1) >= tokens) == (group >= 1)
    first = jnp.where(group == 2, CAP, 0)
    lead_place = jnp.where(mine & (place < CAP), place + first, -2)
    trail_places = [
        jnp.where(mine & (place >= CAP), (place - CAP) * SPLIT + piece + first, -2)
        for piece in range(SPLIT)
    ]

    def matches(places):
        blocks = [
            jnp.where(before[at : at + 1, :] == places, 1.0, 0.0) for at in range(len(order))
        ]
        return jnp.concatenate(blocks, axis=0)

    return matches(lead_place), [matches(places) for places in trail_places], named


def attend(query_ref, key_ref, value_ref, lengths_ref, batch, attn_ref):
    tokens = query_ref.shape[1]
    kv_heads = key_ref.shape[2] // HEAD_WIDTH
    group = query_ref.shape[2] // HEAD_WIDTH // kv_heads
    at_row = row_iota((tokens, tokens), 0)
    at_col = row_iota((tokens, tokens), 1)
    row_request = jnp.zeros((tokens, tokens), jnp.int32)
    col_request = jnp.zeros((tokens, tokens), jnp.int32)
    end = jnp.int32(0)
    for r in range(lengths_ref.shape[2]):
        end = end + lengths_ref[batch, 0, r]
        row_request = row_request + (at_row >= end).astype(jnp.int32)
        col_request = col_request + (at_col >= end).astype(jnp.int32)
    allowed = (row_request == col_request) & (at_col <= at_row)
    bias = jnp.where(allowed, 0.0, -1e30)
    scale = HEAD_WIDTH ** (-0.5) * math.log2(math.e)
    squares = jnp.zeros((tokens, HEAD_WIDTH), F32)
    for h in range(kv_heads):
        kv = slice(h * HEAD_WIDTH, (h + 1) * HEAD_WIDTH)
        heads = [
            slice((h * group + g) * HEAD_WIDTH, (h * group + g + 1) * HEAD_WIDTH)
            for g in range(group)
        ]
        q = jnp.concatenate([query_ref[batch, :, cols] for cols in heads], axis=0)
        scores = dot(q, key_ref[batch, :, kv], ((1,), (1,)))
        scores = scores.reshape(group, tokens, tokens) + bias[None]
        weights = jnp.exp2((scores - jnp.max(scores, axis=-1, keepdims=True)) * scale)
        share = 1.0 / jnp.sum(weights, axis=-1, keepdims=True)
        probs = (weights * share).astype(BF16)
        mixed = dot(probs.reshape(group * tokens, tokens), value_ref[batch, :, kv])
        for g, cols in enumerate(heads):
            part = mixed[g * tokens : (g + 1) * tokens]
            attn_ref[batch, :, cols] = part
            squares = squares + part * part
    meansq = jnp.sum(squares, axis=-1, keepdims=True) / query_ref.shape[2]
    return lax.rsqrt(meansq + 1e-05)


def front_kernel(order, relative, *refs):
    sources, refs = refs[:8], refs[8:]
    if relative:
        gate_hbm, gate_ref, attn_ref, *refs = refs
    else:
        attn_ref, *refs = refs
    send_refs, refs = refs[: -(len(sources) + 2)], refs[-(len(sources) + 2) :]
    *targets, normed_ref, sems = refs
    lengths_ref, holds_ref, dup_ref, routes_ref, gain_ref, query_ref, key_ref, value_ref = targets
    batches, tokens, features = query_ref.shape
    piece, cols = send_refs[0].shape
    step = cols // SPLIT

    small = [pltpu.make_async_copy(sources[i], targets[i], sems.at[0, i]) for i in range(5)]
    large = [
        [
            pltpu.make_async_copy(sources[i].at[b], targets[i].at[b], sems.at[1 + b, i])
            for i in range(5, 8)
        ]
        for b in range(batches)
    ]
    for copy in small + [copy for copies in large for copy in copies]:
        copy.start()
    if relative:
        load = pltpu.make_async_copy(gate_hbm, gate_ref, sems.at[1, 0])
        load.start()
    for copy in small:
        copy.wait()

    @pl.when(holds_ref[0] >= 0)
    def _():
        lead, trail, _ = slot_picks(order, relative, holds_ref, dup_ref, routes_ref)
        for b in range(batches):
            for copy in large[b]:
                copy.wait()
        for b in range(batches):
            scale = attend(query_ref, key_ref, value_ref, lengths_ref, b, attn_ref)
            normed_ref[b * tokens : (b + 1) * tokens, :] = (
                attn_ref[b] * scale * gain_ref[...][None, :]
            ).astype(BF16)
        tail = normed_ref[:, cols:features]
        for j in range(SPLIT):
            at = slice(j * step, (j + 1) * step)
            picks = jnp.concatenate([lead, trail[j]], axis=1).astype(BF16)
            source = jnp.concatenate([normed_ref[:, at], tail], axis=0)
            packed = dot(picks, source)
            for i, send_ref in enumerate(send_refs):
                send_ref[:, at] = packed[i * piece : (i + 1) * piece].astype(BF16)

    if relative:
        load.wait()


def load_kernel(*refs):
    *refs, sems = refs
    half = len(refs) // 2
    loads = [
        pltpu.make_async_copy(refs[i], refs[half + i], sems.at[i]) for i in range(half)
    ]
    for load in loads:
        load.start()
    for load in loads:
        load.wait()


def weights_kernel(order, relative, holds_ref, dup_ref, routes_ref, gates_ref, *mix_refs):
    lead, trail, named = slot_picks(order, relative, holds_ref, dup_ref, routes_ref)
    gates = gates_ref[...]
    gates = jnp.concatenate([gates[:, at, :] for at in range(gates.shape[1])], axis=1)
    gate = jnp.zeros(named[0].shape, F32)
    for k, match in enumerate(named):
        gate = gate + jnp.where(match, gates[k : k + 1, :], 0.0)
    high = gate.astype(BF16).astype(F32)
    lanes = lead.shape[1]
    rows = mix_refs[0].shape[2] // 2
    block = GROUPS * PACK
    for k, part in enumerate((high, gate - high)):
        spread = [jnp.broadcast_to(part[at : at + 1], (block, lanes)) for at in range(len(order))]
        spread = jnp.concatenate(spread, axis=0)
        for j in range(SPLIT):
            for half, pick in enumerate((lead, trail[j])):
                weight = pick * spread
                for i, mix_ref in enumerate(mix_refs):
                    mix_ref[j, half * lanes : (half + 1) * lanes, k * rows : (k + 1) * rows] = (
                        weight[i * rows : (i + 1) * rows].T.astype(BF16)
                    )


def expert_kernel(count, gate_ref, up_ref, down_ref, *rest):
    got_refs, back_refs = rest[:count], rest[count : 2 * count]
    rows_ref, hidden_ref = rest[2 * count :]
    piece, cols = got_refs[0].shape
    features = rows_ref.shape[1]
    step = cols // SPLIT
    block, hidden = hidden_ref.shape
    shape = (block, block)
    row = row_iota(shape, 0)
    other = row_iota(shape, 1)
    place = lax.rem(row, PACK)
    tile = row - place

    def trails(j):
        picked = jnp.zeros(shape, jnp.bool_)
        for a in range(PACK - CAP):
            picked = picked | ((place == a * SPLIT + j) & (other == tile + CAP + a))
        return jnp.where(picked, 1.0, 0.0).astype(BF16)

    take = min(piece, block)
    for start in range(0, piece * count, block):
        spots = [
            (at // piece, slice(at % piece, at % piece + take), slice(at - start, at - start + take))
            for at in range(start, start + block, take)
        ]
        for i, theirs, mine in spots:
            rows_ref[mine, :cols] = got_refs[i][theirs, :]
        tail = jnp.zeros((block, features - cols), F32)
        for j in range(SPLIT):
            tail = tail + dot(trails(j), rows_ref[:, j * step : (j + 1) * step])
        rows_ref[:, cols:] = tail.astype(BF16)
        chunk = 256 if hidden % 256 == 0 else hidden
        for c in range(0, hidden, chunk):
            gate_val = dot(rows_ref[...], gate_ref[0, :, c : c + chunk])
            up_val = dot(rows_ref[...], up_ref[0, :, c : c + chunk])
            hidden_ref[:, c : c + chunk] = (
                gate_val / (1.0 + jnp.exp(-gate_val)) * up_val
            ).astype(BF16)
        tail = dot(hidden_ref[...], down_ref[0, :, cols:]).astype(BF16)
        leading = lax.rem(row_iota((block, step), 0), PACK) < CAP
        for j in range(SPLIT):
            at = slice(j * step, (j + 1) * step)
            moved = dot(trails(j), tail, ((0,), (0,)))
            result = jnp.where(leading, dot(hidden_ref[...], down_ref[0, :, at]), moved)
            for i, theirs, mine in spots:
                back_refs[i][theirs, at] = result[mine].astype(BF16)


def combine_kernel(last, base_ref, mix_ref, *rest):
    if last:
        *back_refs, out_hbm, out_ref, sems = rest
    else:
        *back_refs, out_ref = rest
    batches, tokens, features = base_ref.shape
    lanes = batches * tokens
    piece, cols = back_refs[0].shape
    step = cols // SPLIT
    tail = jnp.zeros((lanes, features - cols), F32)

    def write(index, at):
        return pltpu.make_async_copy(out_ref.at[:, :, at], out_hbm.at[:, :, at], sems.at[index])

    def put(part, index, at):
        for b in range(batches):
            out_ref[b, :, at] = (base_ref[b, :, at] + part[b * tokens : (b + 1) * tokens]).astype(
                out_ref.dtype
            )
        if last:
            write(index, at).start()

    def columns(j):
        return pl.ds(j * step, step)

    for j in range(SPLIT):
        at = columns(j)
        back = jnp.concatenate([back_ref[:, at] for back_ref in back_refs] * 2, axis=0)
        mixed = dot(mix_ref[j], back)
        put(mixed[:lanes], j, at)
        tail = tail + mixed[lanes:]
    rest_at = pl.ds(cols, features - cols)
    put(tail, SPLIT, rest_at)
    if last:
        for j in range(SPLIT):
            write(j, columns(j)).wait()
        write(SPLIT, rest_at).wait()


def results(in_vmem, *shapes):
    kind = pltpu.VMEM if in_vmem else jax.ShapeDtypeStruct
    return [kind(shape, dtype) for shape, dtype in shapes]


def from_hbm(*values):
    return [pltpu.with_memory_space_constraint(value, pltpu.HBM) for value in values]


def in_vmem(count):
    return [pl.BlockSpec(memory_space=pltpu.VMEM)] * count


def in_smem(count):
    return [pl.BlockSpec(memory_space=pltpu.SMEM)] * count


def swap(value, peer):
    if peer == 0:
        return value
    pairs = [(source, source ^ peer) for source in range(lax.axis_size("expert"))]
    return lax.ppermute(value, "expert", pairs)


def after(value, first):
    return lax.optimization_barrier((value, first))[0]


def load_weights(params, *weights):
    return pl.pallas_call(
        load_kernel,
        name="load_weights",
        out_shape=results(True, *[(w.shape, w.dtype) for w in weights]),
        in_specs=[pl.BlockSpec(memory_space=pltpu.HBM)] * len(weights),
        out_specs=in_vmem(len(weights)),
        scratch_shapes=[pltpu.SemaphoreType.DMA((len(weights),))],
        cost_estimate=pl.CostEstimate(
            flops=0, bytes_accessed=sum(w.size * 4 for w in weights), transcendentals=0
        ),
        compiler_params=params,
    )(*from_hbm(*weights))


def exchange_all(value):
    return lax.all_to_all(value, "expert", split_axis=0, concat_axis=0, tiled=True)


def shards(
    query,
    keys,
    values,
    lengths,
    routes,
    gates,
    norm_gain,
    old_holds,
    dup_experts,
    w_gate,
    w_up,
    w_down,
):
    width = lax.axis_size("expert")
    batches, tokens, features = query.shape
    lanes = batches * tokens
    cols = features * CAP // PACK
    hidden = w_gate.shape[2]
    relative = width == PERMUTED_WIDTH
    groups = PEER_GROUPS if relative else [list(range(width))]
    order = [peer for group in groups for peer in group]
    block = GROUPS * PACK
    piece = block if relative else block * width
    counts = [len(group) * block // piece for group in groups]
    params = pltpu.CompilerParams(vmem_limit_bytes=24 * MIB if relative else 56 * MIB)
    routes = jnp.transpose(routes, (2, 0, 1))
    gates = jnp.transpose(gates, (2, 0, 1))

    weight = [(w_gate.shape, w_gate.dtype)] if relative else []
    front_args = from_hbm(
        lengths, old_holds, dup_experts, routes, norm_gain, query, keys, values,
        *[w_gate] * len(weight),
    )
    front = pl.pallas_call(
        functools.partial(front_kernel, order, relative),
        name="attend_and_pack",
        out_shape=results(
            relative,
            *weight,
            ((batches, tokens, features), F32),
            *[((piece, cols), BF16)] * sum(counts),
        ),
        in_specs=[pl.BlockSpec(memory_space=pltpu.HBM)] * len(front_args),
        out_specs=in_vmem(len(weight) + 1 + sum(counts)),
        scratch_shapes=[pltpu.SMEM(x.shape, x.dtype) for x in front_args[:3]]
        + [pltpu.VMEM(x.shape, x.dtype) for x in front_args[3:8]]
        + [pltpu.VMEM((lanes, features), BF16), pltpu.SemaphoreType.DMA((1 + batches, 8))],
        compiler_params=params,
    )(*front_args)
    gate_mat, attn, *send = front if relative else (w_gate, *front)
    sent = dict(zip(order, send))
    arrived = {}
    up_mat, down_mat = w_up, w_down
    if relative:
        half = width // 2
        for peer in groups[0]:
            arrived[peer] = swap(sent[peer], peer)
        up_mat, down_mat = load_weights(params, *[after(w, sent[0]) for w in (w_up, w_down)])
        wait = down_mat
        for peer in groups[1]:
            if peer >= half:
                arrived[peer] = swap(after(sent[peer], wait), peer)
                wait = (down_mat, arrived[groups[0][0]])
        for peer in groups[1]:
            if peer < half:
                arrived[peer] = swap(after(sent[peer], down_mat), peer)
    else:
        arrived[0] = exchange_all(send[0])

    returned = []
    for group, count in zip(groups, counts):
        got = [arrived[peer] for peer in group[:count]]
        rows = min(count * piece, block * 8)
        back = pl.pallas_call(
            functools.partial(expert_kernel, count),
            name="expert_ffn",
            out_shape=results(relative, *[((piece, cols), BF16)] * count),
            in_specs=in_vmem(3 + count),
            out_specs=in_vmem(count),
            scratch_shapes=[pltpu.VMEM((rows, features), BF16), pltpu.VMEM((rows, hidden), BF16)],
            cost_estimate=pl.CostEstimate(
                flops=count * piece * features * hidden * 6,
                bytes_accessed=w_gate.size * 6,
                transcendentals=0,
            ),
            compiler_params=params,
        )(gate_mat, up_mat, down_mat, *got)
        if relative:
            if returned:
                back = [after(back[0], returned[0][0]), *back[1:]]
            returned.append([swap(part, peer) for part, peer in zip(back, group)])
        else:
            returned.append([exchange_all(part) for part in back])

    mixes = pl.pallas_call(
        functools.partial(weights_kernel, order, relative),
        name="gate_weights",
        out_shape=results(
            relative,
            *[((SPLIT, 2 * lanes, 2 * len(group) * block), BF16) for group in groups],
        ),
        in_specs=in_smem(2) + in_vmem(2),
        out_specs=in_vmem(len(groups)),
        cost_estimate=pl.CostEstimate(flops=0, bytes_accessed=4 * MIB, transcendentals=0),
        compiler_params=params,
    )(*from_hbm(old_holds, dup_experts, after(routes, back[0]), gates))

    base = attn
    for at, (mix, back) in enumerate(zip(mixes, returned)):
        last = at == len(groups) - 1
        out = (attn.shape, BF16 if last else F32)
        base = pl.pallas_call(
            functools.partial(combine_kernel, last),
            name="combine",
            out_shape=results(relative and not last, out)[0],
            in_specs=in_vmem(2 + len(back)),
            out_specs=pl.BlockSpec(memory_space=pltpu.HBM) if last else in_vmem(1)[0],
            scratch_shapes=[pltpu.VMEM(*out)] * last
            + [pltpu.SemaphoreType.DMA((SPLIT + 1,))] * last,
            cost_estimate=pl.CostEstimate(
                flops=2 * mix.size * features // SPLIT,
                bytes_accessed=attn.size * 8,
                transcendentals=0,
            ),
            compiler_params=params,
        )(base, mix, *back)
    return base


def solution(mesh):
    placed = (
        P(None, ("dp", "expert"), None),
        P(None, ("dp", "expert"), None),
        P(None, ("dp", "expert"), None),
        P(None, ("dp", "expert"), None),
        P(None, ("dp", "expert"), None),
        P(None, ("dp", "expert"), None),
        P(),
        P(),
        P(),
        P("expert", None, None),
        P("expert", None, None),
        P("expert", None, None),
    )
    return jax.shard_map(
        shards,
        mesh=mesh,
        in_specs=placed,
        out_specs=P(None, ("dp", "expert"), None),
        check_vma=False,
    )
```

```python
import functools
import math

import jax
import jax.numpy as jnp
from jax import lax
from jax.experimental import pallas as pl
from jax.experimental.pallas import tpu as pltpu
from jax.sharding import PartitionSpec as P

HEAD_WIDTH = 128
CAP = 6
PACK = 8
SPLIT = CAP // (PACK - CAP)
GROUPS = 3
PERMUTED_WIDTH = 8
PEER_GROUPS = [[4, 7, 1, 0], [5, 6, 2, 3]]
MIB = 1024 * 1024

F32 = jnp.float32
BF16 = jnp.bfloat16


def dot(a, b, dims=((1,), (0,))):
    return lax.dot_general(a, b, (dims, ((), ())), preferred_element_type=F32)


def row_iota(shape, axis):
    return lax.broadcasted_iota(jnp.int32, shape, axis)


def count_steps(value, step, upto):
    total = jnp.zeros_like(value)
    for at in range(1, upto):
        total = total + (value >= step * at).astype(jnp.int32)
    return total


def slot_picks(order, relative, holds_ref, dup_ref, routes_ref):
    _, batches, tokens = routes_ref.shape
    lanes = batches * tokens
    shape = (len(order), lanes)
    block = row_iota(shape, 0)
    me = lax.axis_index("expert") if relative else 0
    expert = jnp.zeros(shape, jnp.int32)
    for at, slot in enumerate(order):
        expert = jnp.where(block == at, holds_ref[me ^ slot], expert)
    limit = jnp.full(shape, CAP, jnp.int32)
    for at in range(dup_ref.shape[0]):
        limit = jnp.where(expert == dup_ref[at], 2 * CAP, limit)
    limit = jnp.where(row_iota(shape, 1) >= tokens, limit, CAP)
    routes = routes_ref[...]
    routes = jnp.concatenate([routes[:, at, :] for at in range(batches)], axis=1)
    named = [routes[k : k + 1, :] == expert for k in range(routes.shape[0])]
    hit = functools.reduce(jnp.logical_or, named)
    earlier = row_iota((lanes, lanes), 0)
    later = row_iota((lanes, lanes), 1)
    same = (earlier >= tokens) == (later >= tokens)
    before_mat = jnp.where((earlier < later) & same, 1.0, 0.0).astype(BF16)
    before = dot(jnp.where(hit, 1.0, 0.0).astype(BF16), before_mat).astype(jnp.int32)
    before = jnp.where(hit & (before < limit), before, -1)

    shape = (GROUPS * PACK, lanes)
    row = row_iota(shape, 0)
    group = count_steps(row, PACK, GROUPS)
    place = row - group * PACK
    mine = (row_iota(shape, 1) >= tokens) == (group >= 1)
    first = jnp.where(group == 2, CAP, 0)
    lead_place = jnp.where(mine & (place < CAP), place + first, -2)
    trail_places = [
        jnp.where(mine & (place >= CAP), (place - CAP) * SPLIT + piece + first, -2)
        for piece in range(SPLIT)
    ]

    def matches(places):
        blocks = [
            jnp.where(before[at : at + 1, :] == places, 1.0, 0.0) for at in range(len(order))
        ]
        return jnp.concatenate(blocks, axis=0)

    return matches(lead_place), [matches(places) for places in trail_places], named


def attend(query_ref, key_ref, value_ref, lengths_ref, batch, attn_ref):
    tokens = query_ref.shape[1]
    kv_heads = key_ref.shape[2] // HEAD_WIDTH
    group = query_ref.shape[2] // HEAD_WIDTH // kv_heads
    at_row = row_iota((tokens, tokens), 0)
    at_col = row_iota((tokens, tokens), 1)
    row_request = jnp.zeros((tokens, tokens), jnp.int32)
    col_request = jnp.zeros((tokens, tokens), jnp.int32)
    end = jnp.int32(0)
    for r in range(lengths_ref.shape[2]):
        end = end + lengths_ref[batch, 0, r]
        row_request = row_request + (at_row >= end).astype(jnp.int32)
        col_request = col_request + (at_col >= end).astype(jnp.int32)
    allowed = (row_request == col_request) & (at_col <= at_row)
    bias = jnp.where(allowed, 0.0, -1e30)
    scale = HEAD_WIDTH ** (-0.5) * math.log2(math.e)
    squares = jnp.zeros((tokens, HEAD_WIDTH), F32)
    for h in range(kv_heads):
        kv = slice(h * HEAD_WIDTH, (h + 1) * HEAD_WIDTH)
        heads = [
            slice((h * group + g) * HEAD_WIDTH, (h * group + g + 1) * HEAD_WIDTH)
            for g in range(group)
        ]
        q = jnp.concatenate([query_ref[batch, :, cols] for cols in heads], axis=0)
        scores = dot(q, key_ref[batch, :, kv], ((1,), (1,)))
        scores = scores.reshape(group, tokens, tokens) + bias[None]
        weights = jnp.exp2((scores - jnp.max(scores, axis=-1, keepdims=True)) * scale)
        share = 1.0 / jnp.sum(weights, axis=-1, keepdims=True)
        probs = (weights * share).astype(BF16)
        mixed = dot(probs.reshape(group * tokens, tokens), value_ref[batch, :, kv])
        for g, cols in enumerate(heads):
            part = mixed[g * tokens : (g + 1) * tokens]
            attn_ref[batch, :, cols] = part
            squares = squares + part * part
    meansq = jnp.sum(squares, axis=-1, keepdims=True) / query_ref.shape[2]
    return lax.rsqrt(meansq + 1e-05)


def front_kernel(order, relative, *refs):
    sources, refs = refs[:8], refs[8:]
    if relative:
        gate_hbm, gate_ref, attn_ref, *refs = refs
    else:
        attn_ref, *refs = refs
    send_refs, refs = refs[: -(len(sources) + 2)], refs[-(len(sources) + 2) :]
    *targets, normed_ref, sems = refs
    lengths_ref, holds_ref, dup_ref, routes_ref, gain_ref, query_ref, key_ref, value_ref = targets
    batches, tokens, features = query_ref.shape
    piece, cols = send_refs[0].shape
    step = cols // SPLIT

    small = [pltpu.make_async_copy(sources[i], targets[i], sems.at[0, i]) for i in range(5)]
    large = [
        [
            pltpu.make_async_copy(sources[i].at[b], targets[i].at[b], sems.at[1 + b, i])
            for i in range(5, 8)
        ]
        for b in range(batches)
    ]
    for copy in small + [copy for copies in large for copy in copies]:
        copy.start()
    if relative:
        load = pltpu.make_async_copy(gate_hbm, gate_ref, sems.at[1, 0])
        load.start()
    for copy in small:
        copy.wait()

    @pl.when(holds_ref[0] >= 0)
    def _():
        lead, trail, _ = slot_picks(order, relative, holds_ref, dup_ref, routes_ref)
        for b in range(batches):
            for copy in large[b]:
                copy.wait()
        for b in range(batches):
            scale = attend(query_ref, key_ref, value_ref, lengths_ref, b, attn_ref)
            normed_ref[b * tokens : (b + 1) * tokens, :] = (
                attn_ref[b] * scale * gain_ref[...][None, :]
            ).astype(BF16)
        tail = normed_ref[:, cols:features]
        for j in range(SPLIT):
            at = slice(j * step, (j + 1) * step)
            picks = jnp.concatenate([lead, trail[j]], axis=1).astype(BF16)
            source = jnp.concatenate([normed_ref[:, at], tail], axis=0)
            packed = dot(picks, source)
            for i, send_ref in enumerate(send_refs):
                send_ref[:, at] = packed[i * piece : (i + 1) * piece].astype(BF16)

    if relative:
        load.wait()


def load_kernel(*refs):
    *refs, sems = refs
    half = len(refs) // 2
    loads = [
        pltpu.make_async_copy(refs[i], refs[half + i], sems.at[i]) for i in range(half)
    ]
    for load in loads:
        load.start()
    for load in loads:
        load.wait()


def weights_kernel(order, relative, holds_ref, dup_ref, routes_ref, gates_ref, *mix_refs):
    lead, trail, named = slot_picks(order, relative, holds_ref, dup_ref, routes_ref)
    gates = gates_ref[...]
    gates = jnp.concatenate([gates[:, at, :] for at in range(gates.shape[1])], axis=1)
    gate = jnp.zeros(named[0].shape, F32)
    for k, match in enumerate(named):
        gate = gate + jnp.where(match, gates[k : k + 1, :], 0.0)
    high = gate.astype(BF16).astype(F32)
    lanes = lead.shape[1]
    rows = mix_refs[0].shape[2] // 2
    block = GROUPS * PACK
    for k, part in enumerate((high, gate - high)):
        spread = [jnp.broadcast_to(part[at : at + 1], (block, lanes)) for at in range(len(order))]
        spread = jnp.concatenate(spread, axis=0)
        for j in range(SPLIT):
            for half, pick in enumerate((lead, trail[j])):
                weight = pick * spread
                for i, mix_ref in enumerate(mix_refs):
                    mix_ref[j, half * lanes : (half + 1) * lanes, k * rows : (k + 1) * rows] = (
                        weight[i * rows : (i + 1) * rows].T.astype(BF16)
                    )


def expert_kernel(count, gate_ref, up_ref, down_ref, *rest):
    got_refs, back_refs = rest[:count], rest[count : 2 * count]
    rows_ref, hidden_ref = rest[2 * count :]
    piece, cols = got_refs[0].shape
    features = rows_ref.shape[1]
    step = cols // SPLIT
    block, hidden = hidden_ref.shape
    shape = (block, block)
    row = row_iota(shape, 0)
    other = row_iota(shape, 1)
    place = lax.rem(row, PACK)
    tile = row - place

    def trails(j):
        picked = jnp.zeros(shape, jnp.bool_)
        for a in range(PACK - CAP):
            picked = picked | ((place == a * SPLIT + j) & (other == tile + CAP + a))
        return jnp.where(picked, 1.0, 0.0).astype(BF16)

    take = min(piece, block)
    for start in range(0, piece * count, block):
        spots = [
            (at // piece, slice(at % piece, at % piece + take), slice(at - start, at - start + take))
            for at in range(start, start + block, take)
        ]
        for i, theirs, mine in spots:
            rows_ref[mine, :cols] = got_refs[i][theirs, :]
        tail = jnp.zeros((block, features - cols), F32)
        for j in range(SPLIT):
            tail = tail + dot(trails(j), rows_ref[:, j * step : (j + 1) * step])
        rows_ref[:, cols:] = tail.astype(BF16)
        chunk = 256 if hidden % 256 == 0 else hidden
        for c in range(0, hidden, chunk):
            gate_val = dot(rows_ref[...], gate_ref[0, :, c : c + chunk])
            up_val = dot(rows_ref[...], up_ref[0, :, c : c + chunk])
            hidden_ref[:, c : c + chunk] = (
                gate_val / (1.0 + jnp.exp(-gate_val)) * up_val
            ).astype(BF16)
        tail = dot(hidden_ref[...], down_ref[0, :, cols:]).astype(BF16)
        leading = lax.rem(row_iota((block, step), 0), PACK) < CAP
        for j in range(SPLIT):
            at = slice(j * step, (j + 1) * step)
            moved = dot(trails(j), tail, ((0,), (0,)))
            result = jnp.where(leading, dot(hidden_ref[...], down_ref[0, :, at]), moved)
            for i, theirs, mine in spots:
                back_refs[i][theirs, at] = result[mine].astype(BF16)


def combine_kernel(last, base_ref, mix_ref, *rest):
    if last:
        *back_refs, out_hbm, out_ref, sems = rest
    else:
        *back_refs, out_ref = rest
    batches, tokens, features = base_ref.shape
    lanes = batches * tokens
    piece, cols = back_refs[0].shape
    step = cols // SPLIT
    tail = jnp.zeros((lanes, features - cols), F32)

    def write(index, at):
        return pltpu.make_async_copy(out_ref.at[:, :, at], out_hbm.at[:, :, at], sems.at[index])

    def put(part, index, at):
        for b in range(batches):
            out_ref[b, :, at] = (base_ref[b, :, at] + part[b * tokens : (b + 1) * tokens]).astype(
                out_ref.dtype
            )
        if last:
            write(index, at).start()

    def columns(j):
        return pl.ds(j * step, step)

    for j in range(SPLIT):
        at = columns(j)
        back = jnp.concatenate([back_ref[:, at] for back_ref in back_refs] * 2, axis=0)
        mixed = dot(mix_ref[j], back)
        put(mixed[:lanes], j, at)
        tail = tail + mixed[lanes:]
    rest_at = pl.ds(cols, features - cols)
    put(tail, SPLIT, rest_at)
    if last:
        for j in range(SPLIT):
            write(j, columns(j)).wait()
        write(SPLIT, rest_at).wait()


def results(in_vmem, *shapes):
    kind = pltpu.VMEM if in_vmem else jax.ShapeDtypeStruct
    return [kind(shape, dtype) for shape, dtype in shapes]


def from_hbm(*values):
    return [pltpu.with_memory_space_constraint(value, pltpu.HBM) for value in values]


def in_vmem(count):
    return [pl.BlockSpec(memory_space=pltpu.VMEM)] * count


def in_smem(count):
    return [pl.BlockSpec(memory_space=pltpu.SMEM)] * count


def swap(value, peer):
    if peer == 0:
        return value
    pairs = [(source, source ^ peer) for source in range(lax.axis_size("expert"))]
    return lax.ppermute(value, "expert", pairs)


def after(value, first):
    return lax.optimization_barrier((value, first))[0]


def load_weights(params, *weights):
    return pl.pallas_call(
        load_kernel,
        name="load_weights",
        out_shape=results(True, *[(w.shape, w.dtype) for w in weights]),
        in_specs=[pl.BlockSpec(memory_space=pltpu.HBM)] * len(weights),
        out_specs=in_vmem(len(weights)),
        scratch_shapes=[pltpu.SemaphoreType.DMA((len(weights),))],
        cost_estimate=pl.CostEstimate(
            flops=0, bytes_accessed=sum(w.size * 4 for w in weights), transcendentals=0
        ),
        compiler_params=params,
    )(*from_hbm(*weights))


def exchange_all(value):
    return lax.all_to_all(value, "expert", split_axis=0, concat_axis=0, tiled=True)


def shards(
    query,
    keys,
    values,
    lengths,
    routes,
    gates,
    norm_gain,
    old_holds,
    dup_experts,
    w_gate,
    w_up,
    w_down,
):
    width = lax.axis_size("expert")
    batches, tokens, features = query.shape
    lanes = batches * tokens
    cols = features * CAP // PACK
    hidden = w_gate.shape[2]
    relative = width == PERMUTED_WIDTH
    groups = PEER_GROUPS if relative else [list(range(width))]
    order = [peer for group in groups for peer in group]
    block = GROUPS * PACK
    piece = block if relative else block * width
    counts = [len(group) * block // piece for group in groups]
    params = pltpu.CompilerParams(vmem_limit_bytes=24 * MIB if relative else 56 * MIB)
    routes = jnp.transpose(routes, (2, 0, 1))
    gates = jnp.transpose(gates, (2, 0, 1))

    weight = [(w_gate.shape, w_gate.dtype)] if relative else []
    front_args = from_hbm(
        lengths, old_holds, dup_experts, routes, norm_gain, query, keys, values,
        *[w_gate] * len(weight),
    )
    front = pl.pallas_call(
        functools.partial(front_kernel, order, relative),
        name="attend_and_pack",
        out_shape=results(
            relative,
            *weight,
            ((batches, tokens, features), F32),
            *[((piece, cols), BF16)] * sum(counts),
        ),
        in_specs=[pl.BlockSpec(memory_space=pltpu.HBM)] * len(front_args),
        out_specs=in_vmem(len(weight) + 1 + sum(counts)),
        scratch_shapes=[pltpu.SMEM(x.shape, x.dtype) for x in front_args[:3]]
        + [pltpu.VMEM(x.shape, x.dtype) for x in front_args[3:8]]
        + [pltpu.VMEM((lanes, features), BF16), pltpu.SemaphoreType.DMA((1 + batches, 8))],
        compiler_params=params,
    )(*front_args)
    gate_mat, attn, *send = front if relative else (w_gate, *front)
    sent = dict(zip(order, send))
    arrived = {}
    up_mat, down_mat = w_up, w_down
    if relative:
        half = width // 2
        for peer in groups[0]:
            arrived[peer] = swap(sent[peer], peer)
        up_mat, down_mat = load_weights(params, *[after(w, sent[0]) for w in (w_up, w_down)])
        wait = down_mat
        for peer in groups[1]:
            if peer >= half:
                arrived[peer] = swap(after(sent[peer], wait), peer)
                wait = (down_mat, arrived[groups[0][0]])
        for peer in groups[1]:
            if peer < half:
                arrived[peer] = swap(after(sent[peer], down_mat), peer)
    else:
        arrived[0] = exchange_all(send[0])

    returned = []
    for group, count in zip(groups, counts):
        got = [arrived[peer] for peer in group[:count]]
        rows = min(count * piece, block * 8)
        back = pl.pallas_call(
            functools.partial(expert_kernel, count),
            name="expert_ffn",
            out_shape=results(relative, *[((piece, cols), BF16)] * count),
            in_specs=in_vmem(3 + count),
            out_specs=in_vmem(count),
            scratch_shapes=[pltpu.VMEM((rows, features), BF16), pltpu.VMEM((rows, hidden), BF16)],
            cost_estimate=pl.CostEstimate(
                flops=count * piece * features * hidden * 6,
                bytes_accessed=w_gate.size * 6,
                transcendentals=0,
            ),
            compiler_params=params,
        )(gate_mat, up_mat, down_mat, *got)
        if relative:
            returned.append([swap(part, peer) for part, peer in zip(back, group)])
        else:
            returned.append([exchange_all(part) for part in back])

    mixes = pl.pallas_call(
        functools.partial(weights_kernel, order, relative),
        name="gate_weights",
        out_shape=results(
            relative,
            *[((SPLIT, 2 * lanes, 2 * len(group) * block), BF16) for group in groups],
        ),
        in_specs=in_smem(2) + in_vmem(2),
        out_specs=in_vmem(len(groups)),
        cost_estimate=pl.CostEstimate(flops=0, bytes_accessed=4 * MIB, transcendentals=0),
        compiler_params=params,
    )(*from_hbm(old_holds, dup_experts, after(routes, arrived[groups[0][0]]), gates))

    base = attn
    for at, (mix, back) in enumerate(zip(mixes, returned)):
        last = at == len(groups) - 1
        out = (attn.shape, BF16 if last else F32)
        base = pl.pallas_call(
            functools.partial(combine_kernel, last),
            name="combine",
            out_shape=results(relative and not last, out)[0],
            in_specs=in_vmem(2 + len(back)),
            out_specs=pl.BlockSpec(memory_space=pltpu.HBM) if last else in_vmem(1)[0],
            scratch_shapes=[pltpu.VMEM(*out)] * last
            + [pltpu.SemaphoreType.DMA((SPLIT + 1,))] * last,
            cost_estimate=pl.CostEstimate(
                flops=2 * mix.size * features // SPLIT,
                bytes_accessed=attn.size * 8,
                transcendentals=0,
            ),
            compiler_params=params,
        )(base, mix, *back)
    return base


def solution(mesh):
    placed = (
        P(None, ("dp", "expert"), None),
        P(None, ("dp", "expert"), None),
        P(None, ("dp", "expert"), None),
        P(None, ("dp", "expert"), None),
        P(None, ("dp", "expert"), None),
        P(None, ("dp", "expert"), None),
        P(),
        P(),
        P(),
        P("expert", None, None),
        P("expert", None, None),
        P("expert", None, None),
    )
    return jax.shard_map(
        shards,
        mesh=mesh,
        in_specs=placed,
        out_specs=P(None, ("dp", "expert"), None),
        check_vma=False,
    )
```
